32 devices in a mesh: head: 2 (over y), inner: 4 (over x, core), outer: 4 (over z).
Axes of the slice: x: 2, y: 2, z: 4, core: 2. Of those that a mesh axis runs over, the one named last changes fastest.
Arguments:
- query: bfloat16 [4, 4, 256, 4096], P('outer', 'inner', 'head'), may hold values from -300 to 300
- dout: bfloat16 [4, 4, 256, 4096], P('outer', 'inner', 'head'), may hold values from -6 to 6
- key_mant: bfloat16 [4, 4, 256, 512], P('outer', 'inner', None, 'head'), may hold values from -6 to 6
- value_mantissas: bfloat16 [4, 4, 256, 512], P('outer', 'inner', None, 'head'), may hold values from -6 to 6
- key_exps: int32 [4, 4, 2, 4], P('outer', 'inner', None, 'head'), may hold values from -1 to 1
- value_exponents: int32 [4, 4, 2, 4], P('outer', 'inner', None, 'head'), may hold values from -1 to 1
- reach: int32 [4, 4], P('outer', 'inner'), may hold values from 64 to 256
Outputs:
- query_grad: bfloat16 [4, 4, 256, 4096], P('outer', 'inner', 'head')
- key_grad: bfloat16 [4, 4, 256, 512], P('outer', 'inner', None, 'head')
- value_grad: bfloat16 [4, 4, 256, 512], P('outer', 'inner', None, 'head')
The draws below stay inside these ranges and needn't reach their ends.
All inputs are finite; a program needn't handle non-finite values.
Results may differ from the reference program's by a relative error of at most 0.013.
Values may be sent and summed in bfloat16 or wider, within the bound.
A program may use at most 64 MiB of HBM per device.

```python
import jax
import jax.numpy as jnp
from jax import lax

QUERY_HEADS = 32
KEY_VALUE_HEADS = 4
HEAD_SIZE = 128
ROWS_PER_SCALE = 128
BLOCK_TOKENS = 256
BLOCKS_PER_GROUP = 4
BLOCK_GROUPS = 4


def shared_keys(key):
    mantissa_values = jax.random.truncated_normal(jax.random.fold_in(key, 101), -6.0, 6.0, (BLOCK_GROUPS, BLOCKS_PER_GROUP, BLOCK_TOKENS, KEY_VALUE_HEADS * HEAD_SIZE), jnp.float32)
    scale_exponents = jax.random.randint(jax.random.fold_in(key, 102), (BLOCK_GROUPS, BLOCKS_PER_GROUP, BLOCK_TOKENS // ROWS_PER_SCALE, KEY_VALUE_HEADS), -1, 2)
    return (mantissa_values, scale_exponents)


def draw_key_exps(key, part):
    mantissa_values, scale_exponents = shared_keys(key)
    return scale_exponents.astype(jnp.int32)


def draw_key_mant(key, part):
    mantissa_values, scale_exponents = shared_keys(key)
    return mantissa_values.astype(jnp.bfloat16)


def draw_query(key, part):
    key = jax.random.fold_in(key, 7)
    block_values = jax.random.truncated_normal(jax.random.fold_in(key, 1), -6.0, 6.0, (BLOCK_GROUPS, BLOCKS_PER_GROUP, BLOCK_TOKENS, QUERY_HEADS * HEAD_SIZE), jnp.float32)
    return block_values.astype(jnp.bfloat16)


def place_ends(drawn, key, least, largest):
    dims = drawn.shape
    spot = [jax.random.randint(jax.random.fold_in(key, axis), (), 0, dims[axis]) for axis in range(len(dims))]
    drawn = drawn.at[tuple(spot)].set(least)
    longest = dims.index(max(dims))
    spot[longest] = (spot[longest] + 1) % dims[longest]
    return drawn.at[tuple(spot)].set(largest)


def steps_of(rng, shape, shards, low, top_value):
    gain, own = 1.0, jax.random.fold_in(rng, 6)
    for axis_at, blocks in shards:
        heights = jnp.exp(jax.random.uniform(jax.random.fold_in(own, axis_at), (blocks,), jnp.float32, low / len(shards), top_value / len(shards)))
        gain = gain * jnp.repeat(heights, shape[axis_at] // blocks).reshape([-1 if axis == axis_at else 1 for axis in range(len(shape))])
    return gain


def centred(stream_key, shape, spread, most, cuts=(), dtype=jnp.bfloat16):
    level = steps_of(stream_key, shape, cuts, -0.22, 0.18) if cuts else 1.0
    result = jax.random.normal(stream_key, shape, jnp.float32) * spread * level
    return jnp.minimum(jnp.maximum(result, -most), most).astype(dtype)


def setup_inputs(seed: int = 0) -> dict:
    key_list = jax.random.split(jax.random.key(seed), 8)
    return {
        "query": draw_query(jax.random.fold_in(key_list[7], 71), 0),
        "dout": centred(key_list[1], (BLOCK_GROUPS, BLOCKS_PER_GROUP, BLOCK_TOKENS, QUERY_HEADS * HEAD_SIZE), 1.0, 6.0, ((0, 4), (1, 4), (2, 2))),
        "key_mant": draw_key_mant(jax.random.fold_in(key_list[7], 71), 0),
        "value_mantissas": centred(key_list[3], (BLOCK_GROUPS, BLOCKS_PER_GROUP, BLOCK_TOKENS, KEY_VALUE_HEADS * HEAD_SIZE), 1.0, 6.0, ((0, 4), (1, 4), (3, 2))),
        "key_exps": draw_key_exps(jax.random.fold_in(key_list[7], 71), 0),
        "value_exponents": place_ends(jax.random.randint(key_list[5], (BLOCK_GROUPS, BLOCKS_PER_GROUP, BLOCK_TOKENS // ROWS_PER_SCALE, KEY_VALUE_HEADS), -1, 2), jax.random.fold_in(key_list[5], 1), -1, 1).astype(jnp.int32),
        "reach": place_ends(jax.random.randint(key_list[6], (BLOCK_GROUPS, BLOCKS_PER_GROUP), BLOCK_TOKENS // 4, BLOCK_TOKENS + 1), jax.random.fold_in(key_list[6], 1), BLOCK_TOKENS // 4, BLOCK_TOKENS).astype(jnp.int32),
    }


NEG_FILL = -1e30


def dequant(mantissa_values, scale_exponents):
    reshaped_array = mantissa_values.astype(jnp.float32).reshape(BLOCK_GROUPS, BLOCKS_PER_GROUP, BLOCK_TOKENS // ROWS_PER_SCALE, ROWS_PER_SCALE, KEY_VALUE_HEADS, HEAD_SIZE)
    scale_factors = jnp.exp2(scale_exponents.astype(jnp.float32))[:, :, :, None, :, None]
    return (reshaped_array * scale_factors).astype(jnp.bfloat16).reshape(BLOCK_GROUPS, BLOCKS_PER_GROUP, BLOCK_TOKENS, KEY_VALUE_HEADS, HEAD_SIZE)


def one_block(members):
    query_matrix, gradient_rows, key_own, value_own, key_prev, value_prev, reach_rows, first_cycle = members
    heads_per_group = QUERY_HEADS // KEY_VALUE_HEADS
    factor = HEAD_SIZE ** -0.5
    query_complete = query_matrix.reshape(BLOCK_TOKENS, KEY_VALUE_HEADS, heads_per_group, HEAD_SIZE).astype(jnp.float32)
    gradient_complete = gradient_rows.reshape(BLOCK_TOKENS, KEY_VALUE_HEADS, heads_per_group, HEAD_SIZE).astype(jnp.float32)
    key_all = jnp.concatenate([key_prev, key_own], axis=0).astype(jnp.float32)
    value_all = jnp.concatenate([value_prev, value_own], axis=0).astype(jnp.float32)
    scores = jnp.einsum("tkgd,skd->kgts", query_complete, key_all) * factor
    columns = jnp.arange(2 * BLOCK_TOKENS)
    positions = jnp.arange(BLOCK_TOKENS)
    prev_mask = (columns < BLOCK_TOKENS) & (columns >= BLOCK_TOKENS - reach_rows) & jnp.logical_not(first_cycle)
    own_mask = (columns[None, :] >= BLOCK_TOKENS) & (columns[None, :] - BLOCK_TOKENS <= positions[:, None])
    visible = own_mask | prev_mask[None, :]
    scores = jnp.where(visible[None, None], scores, NEG_FILL)
    row_peak = jnp.max(scores, axis=3, keepdims=True)
    weights = jnp.exp(scores - row_peak)
    probs = weights / jnp.sum(weights, axis=3, keepdims=True)
    rounded = lax.optimization_barrier(probs.astype(jnp.bfloat16)).astype(jnp.float32)
    output = jnp.einsum("kgts,skd->kgtd", rounded, value_all)
    row_dot = jnp.einsum("tkgd,kgtd->kgt", gradient_complete, output)
    dprob = jnp.einsum("tkgd,skd->kgts", gradient_complete, value_all)
    dscore = lax.optimization_barrier((probs * (dprob - row_dot[..., None])).astype(jnp.bfloat16)).astype(jnp.float32)
    query_grad = (jnp.einsum("kgts,skd->tkgd", dscore, key_all) * factor).astype(jnp.bfloat16)
    key_terms = jnp.einsum("kgts,tkgd->skd", dscore, query_complete) * factor
    value_terms = jnp.einsum("kgts,tkgd->skd", rounded, gradient_complete)
    return (query_grad.reshape(BLOCK_TOKENS, QUERY_HEADS * HEAD_SIZE), key_terms[BLOCK_TOKENS:], value_terms[BLOCK_TOKENS:],
            key_terms[:BLOCK_TOKENS], value_terms[:BLOCK_TOKENS])


def reference(query, dout, key_mant, value_mantissas, key_exps, value_exponents, reach):
    block_keys = dequant(key_mant, key_exps)
    block_values = dequant(value_mantissas, value_exponents)
    predecessor_keys = jnp.concatenate([jnp.zeros_like(block_keys[:, :1]), block_keys[:, :-1]], axis=1)
    predecessor_values = jnp.concatenate([jnp.zeros_like(block_values[:, :1]), block_values[:, :-1]], axis=1)
    first_flags = jnp.broadcast_to(jnp.arange(BLOCKS_PER_GROUP)[None, :] == 0, (BLOCK_GROUPS, BLOCKS_PER_GROUP))
    item_count = BLOCK_GROUPS * BLOCKS_PER_GROUP
    members = (query.reshape(item_count, BLOCK_TOKENS, QUERY_HEADS * HEAD_SIZE), dout.reshape(item_count, BLOCK_TOKENS, QUERY_HEADS * HEAD_SIZE),
               block_keys.reshape(item_count, BLOCK_TOKENS, KEY_VALUE_HEADS, HEAD_SIZE), block_values.reshape(item_count, BLOCK_TOKENS, KEY_VALUE_HEADS, HEAD_SIZE),
               predecessor_keys.reshape(item_count, BLOCK_TOKENS, KEY_VALUE_HEADS, HEAD_SIZE), predecessor_values.reshape(item_count, BLOCK_TOKENS, KEY_VALUE_HEADS, HEAD_SIZE),
               reach.reshape(item_count), first_flags.reshape(item_count))
    query_grad, key_own, value_own, key_next, value_next = lax.map(one_block, members)
    key_value_shape = (BLOCK_GROUPS, BLOCKS_PER_GROUP, BLOCK_TOKENS, KEY_VALUE_HEADS, HEAD_SIZE)
    key_next = lax.optimization_barrier(key_next.reshape(key_value_shape).astype(jnp.bfloat16)).astype(jnp.float32)
    value_next = lax.optimization_barrier(value_next.reshape(key_value_shape).astype(jnp.bfloat16)).astype(jnp.float32)
    key_next = jnp.concatenate([key_next[:, 1:], jnp.zeros_like(key_next[:, :1])], axis=1)
    value_next = jnp.concatenate([value_next[:, 1:], jnp.zeros_like(value_next[:, :1])], axis=1)
    key_grad = (key_own.reshape(key_value_shape) + key_next).astype(jnp.bfloat16)
    value_grad = (value_own.reshape(key_value_shape) + value_next).astype(jnp.bfloat16)
    output_shape = (BLOCK_GROUPS, BLOCKS_PER_GROUP, BLOCK_TOKENS, KEY_VALUE_HEADS * HEAD_SIZE)
    return (query_grad.reshape(BLOCK_GROUPS, BLOCKS_PER_GROUP, BLOCK_TOKENS, QUERY_HEADS * HEAD_SIZE), key_grad.reshape(output_shape),
            value_grad.reshape(output_shape))
```

```python
import functools

import jax
import jax.numpy as jnp
from jax import lax
from jax.experimental import pallas as pl
from jax.experimental.pallas import tpu as pltpu
from jax.sharding import PartitionSpec as P

D = 128
GROUP = 8
LOG2E = 1.4426950408889634
NEG_FILL = -1e30
F32 = jnp.float32
BF16 = jnp.bfloat16
MESH = pl.DeviceIdType.MESH


def scale_of(exponent):
    return jnp.where(exponent > 0, 2.0, jnp.where(exponent < 0, 0.5, 1.0)).astype(F32)


def kernel(
    ring,
    q_hbm,
    do_hbm,
    km_ref,
    vm_ref,
    ke_ref,
    ve_ref,
    reach_ref,
    dq_hbm,
    dk_ref,
    dv_ref,
    q_s,
    do_s,
    dq_s,
    kv,
    bias,
    p_s,
    ds_s,
    own,
    gsend,
    grecv,
    fsend,
    frecv,
    q_sem,
    do_sem,
    dq_sem,
    a_send,
    a_recv,
    b_send,
    b_recv,
    d_send,
    d_recv,
    f_send,
    f_recv,
):
    rows = q_s.shape[1]
    length = km_ref.shape[2]
    width = q_s.shape[2]
    mine = km_ref.shape[3] // D
    heads = 2 * mine
    factor = D**-0.5

    h = lax.axis_index("head")
    r = lax.axis_index("inner")
    other = 1 - h
    has_prev = r > 0
    has_next = r < ring - 1

    def columns(slot):
        return pl.ds(pl.multiple_of(lax.rem(mine * h + slot, heads) * width, width), width)

    def load_q(slot):
        return pltpu.make_async_copy(q_hbm.at[0, 0, :, columns(slot)], q_s.at[slot], q_sem.at[slot])

    def load_do(slot):
        return pltpu.make_async_copy(
            do_hbm.at[0, 0, :, columns(slot)], do_s.at[slot], do_sem.at[slot]
        )

    def store_dq(slot):
        return pltpu.make_async_copy(
            dq_s.at[slot], dq_hbm.at[0, 0, :, columns(slot)], dq_sem.at[slot]
        )

    def copy_a(j):
        return pltpu.make_async_remote_copy(
            src_ref=kv.at[j, :, pl.ds(length, length)],
            dst_ref=kv.at[mine + j, :, pl.ds(length, length)],
            send_sem=a_send.at[j],
            recv_sem=a_recv.at[j],
            device_id={"head": other},
            device_id_type=MESH,
        )

    def copy_b(slot):
        return pltpu.make_async_remote_copy(
            src_ref=kv.at[slot, :, pl.ds(length, length)],
            dst_ref=kv.at[slot, :, pl.ds(0, length)],
            send_sem=b_send.at[slot],
            recv_sem=b_recv.at[slot],
            device_id={"inner": r + 1},
            device_id_type=MESH,
        )

    def copy_d(slot):
        return pltpu.make_async_remote_copy(
            src_ref=gsend.at[slot],
            dst_ref=grecv.at[slot],
            send_sem=d_send.at[slot],
            recv_sem=d_recv.at[slot],
            device_id={"inner": r - 1},
            device_id_type=MESH,
        )

    def copy_f(j):
        return pltpu.make_async_remote_copy(
            src_ref=fsend.at[j],
            dst_ref=frecv.at[j],
            send_sem=f_send.at[j],
            recv_sem=f_recv.at[j],
            device_id={"head": other},
            device_id_type=MESH,
        )

    barrier = pltpu.get_barrier_semaphore()
    pl.semaphore_signal(barrier, inc=1, device_id={"head": other}, device_id_type=MESH)

    @pl.when(has_prev)
    def _():
        pl.semaphore_signal(barrier, inc=1, device_id={"inner": r - 1}, device_id_type=MESH)

    @pl.when(has_next)
    def _():
        pl.semaphore_signal(barrier, inc=1, device_id={"inner": r + 1}, device_id_type=MESH)

    for slot in range(heads):
        load_q(slot).start()
        load_do(slot).start()

    half = length // 2
    for j in range(mine):
        for b in range(2):
            for which, mant, exps in ((0, km_ref, ke_ref), (1, vm_ref, ve_ref)):
                block = mant[0, 0, b * half : (b + 1) * half, j * D : (j + 1) * D].astype(F32)
                kv[j, which, length + b * half : length + (b + 1) * half, :] = (
                    block * scale_of(exps[0, 0, b, j])
                ).astype(BF16)

    pl.semaphore_wait(barrier, 1 + has_prev.astype(jnp.int32) + has_next.astype(jnp.int32))

    for j in range(mine):
        copy_a(j).start()

        @pl.when(has_next)
        def _():
            copy_b(j).start()

    key_at = lax.broadcasted_iota(jnp.int32, (length, 2 * rows), 0)
    query_at = lax.rem(lax.broadcasted_iota(jnp.int32, (length, 2 * rows), 1), rows) + h * rows
    first_seen = jnp.where(has_prev, length - reach_ref[0, 0], length)
    bias[0:length, :] = jnp.where(key_at >= first_seen, 0.0, NEG_FILL).astype(F32)
    bias[length : 2 * length, :] = jnp.where(key_at <= query_at, 0.0, NEG_FILL).astype(F32)

    @pl.when(jnp.logical_not(has_prev))
    def _():
        for slot in range(heads):
            kv[slot, :, 0:length, :] = jnp.zeros((2, length, D), BF16)

    @pl.when(jnp.logical_not(has_next))
    def _():
        grecv[...] = jnp.zeros_like(grecv)

    def finish(j):
        @pl.when(has_next)
        def _():
            copy_d(mine + j).wait_recv()

        fsend[j] = (own[mine + j] + grecv[mine + j].astype(F32)).astype(BF16)
        copy_f(j).start()

    def one_slot(slot, carry):
        load_q(slot).wait()
        load_do(slot).wait()

        for j in range(mine):
            @pl.when(slot == j + 1)
            def _():
                copy_a(j).wait_recv()

                @pl.when(has_next)
                def _():
                    copy_b(mine + j).start()

        @pl.when(has_prev)
        def _():
            copy_b(slot).wait_recv()

        keys = kv[slot, 0]
        values = kv[slot, 1]
        keys_t = keys.T
        q_list, do_list = [], []
        for pair in range(GROUP // 2):
            at = pair * 2 * D
            q_pair = jnp.concatenate(
                [q_s[slot, :, at : at + D], q_s[slot, :, at + D : at + 2 * D]], axis=0
            )
            do_pair = jnp.concatenate(
                [do_s[slot, :, at : at + D], do_s[slot, :, at + D : at + 2 * D]], axis=0
            )
            q_list.append(q_pair)
            do_list.append(do_pair)
            contract = (((1,), (1,)), ((), ()))
            scores = lax.dot_general(keys, q_pair, contract, preferred_element_type=F32)
            scores = scores * (factor * LOG2E) + bias[...]
            peak = jnp.max(scores, axis=0, keepdims=True)
            weights = jnp.exp2(scores - peak)
            total = jnp.sum(weights, axis=0, keepdims=True)
            probs = weights * (1.0 / total)
            rounded = probs.astype(BF16)
            dprob = lax.dot_general(values, do_pair, contract, preferred_element_type=F32)
            row_dot = jnp.sum(rounded.astype(F32) * dprob, axis=0, keepdims=True)
            dscore = (probs * (dprob - row_dot)).astype(BF16)
            span = slice(pair * 2 * rows, (pair + 1) * 2 * rows)
            p_s[:, span] = rounded
            ds_s[:, span] = dscore
            grad_t = jnp.dot(keys_t, dscore, preferred_element_type=F32) * factor
            dq_s[slot, :, at : at + D] = grad_t[:, :rows].T.astype(BF16)
            dq_s[slot, :, at + D : at + 2 * D] = grad_t[:, rows:].T.astype(BF16)
        store_dq(slot).start()

        @pl.when(slot == mine + 1)
        def _():
            finish(0)

        dv = jnp.dot(p_s[...], jnp.concatenate(do_list, axis=0), preferred_element_type=F32)
        dk = jnp.dot(ds_s[...], jnp.concatenate(q_list, axis=0), preferred_element_type=F32) * factor
        gsend[slot, 0] = dk[:length].astype(BF16)
        gsend[slot, 1] = dv[:length].astype(BF16)

        @pl.when(has_prev)
        def _():
            copy_d(slot).start()

        own[slot, 0] = dk[length:]
        own[slot, 1] = dv[length:]
        return carry

    lax.fori_loop(0, heads, one_slot, 0)
    for j in range(1, mine):
        finish(j)

    for j in range(mine):

        @pl.when(has_next)
        def _():
            copy_d(j).wait_recv()

        copy_f(j).wait_recv()
        total = own[j] + grecv[j].astype(F32) + frecv[j].astype(F32)
        dk_ref[0, 0, :, j * D : (j + 1) * D] = total[0].astype(BF16)
        dv_ref[0, 0, :, j * D : (j + 1) * D] = total[1].astype(BF16)

    for j in range(mine):
        copy_a(j).wait_send()
        copy_f(j).wait_send()
    for slot in range(heads):
        store_dq(slot).wait()

        @pl.when(has_next)
        def _():
            copy_b(slot).wait_send()

        @pl.when(has_prev)
        def _():
            copy_d(slot).wait_send()


def on_device(ring, query, dout, key_mant, value_mantissas, key_exps, value_exponents, reach):
    rows, length = query.shape[2], key_mant.shape[2]
    mine = key_mant.shape[3] // D
    heads = 2 * mine
    width = GROUP * D
    hbm = pl.BlockSpec(memory_space=pl.ANY)
    vmem = pl.BlockSpec(memory_space=pltpu.VMEM)
    smem = pl.BlockSpec(memory_space=pltpu.SMEM)
    dma = pltpu.SemaphoreType.DMA
    return pl.pallas_call(
        functools.partial(kernel, ring),
        out_shape=(
            jax.ShapeDtypeStruct(query.shape, BF16),
            jax.ShapeDtypeStruct(key_mant.shape, BF16),
            jax.ShapeDtypeStruct(key_mant.shape, BF16),
        ),
        in_specs=[hbm, hbm, vmem, vmem, smem, smem, smem],
        out_specs=(hbm, vmem, vmem),
        scratch_shapes=[
            pltpu.VMEM((heads, rows, width), BF16),
            pltpu.VMEM((heads, rows, width), BF16),
            pltpu.VMEM((heads, rows, width), BF16),
            pltpu.VMEM((heads, 2, 2 * length, D), BF16),
            pltpu.VMEM((2 * length, 2 * rows), F32),
            pltpu.VMEM((2 * length, GROUP * rows), BF16),
            pltpu.VMEM((2 * length, GROUP * rows), BF16),
            pltpu.VMEM((heads, 2, length, D), F32),
            pltpu.VMEM((heads, 2, length, D), BF16),
            pltpu.VMEM((heads, 2, length, D), BF16),
            pltpu.VMEM((mine, 2, length, D), BF16),
            pltpu.VMEM((mine, 2, length, D), BF16),
            dma((heads,)),
            dma((heads,)),
            dma((heads,)),
            dma((mine,)),
            dma((mine,)),
            dma((heads,)),
            dma((heads,)),
            dma((heads,)),
            dma((heads,)),
            dma((mine,)),
            dma((mine,)),
        ],
        compiler_params=pltpu.CompilerParams(
            collective_id=0, has_side_effects=True, vmem_limit_bytes=48 * 2**20
        ),
        cost_estimate=pl.CostEstimate(
            flops=10 * heads * width * rows * 2 * length,
            bytes_accessed=6 * rows * heads * width,
            transcendentals=heads * GROUP * rows * 2 * length,
        ),
    )(query, dout, key_mant, value_mantissas, key_exps, value_exponents, reach)


def solution(mesh):
    assert mesh.shape["head"] == 2
    tokens = P("outer", "inner", "head", None)
    shared = P("outer", "inner", None, "head")
    return jax.shard_map(
        functools.partial(on_device, mesh.shape["inner"]),
        mesh=mesh,
        in_specs=(tokens, tokens, shared, shared, shared, shared, P("outer", "inner")),
        out_specs=(tokens, shared, shared),
        check_vma=False,
    )
```

```python
import functools

import jax
import jax.numpy as jnp
from jax import lax
from jax.experimental import pallas as pl
from jax.experimental.pallas import tpu as pltpu
from jax.sharding import PartitionSpec as P

D = 128
GROUP = 8
LOG2E = 1.4426950408889634
NEG_FILL = -1e30
F32 = jnp.float32
BF16 = jnp.bfloat16
MESH = pl.DeviceIdType.MESH


def scale_of(exponent):
    return jnp.where(exponent > 0, 2.0, jnp.where(exponent < 0, 0.5, 1.0)).astype(F32)


def kernel(
    ring,
    q_hbm,
    do_hbm,
    km_hbm,
    vm_hbm,
    ke_hbm,
    ve_hbm,
    reach_hbm,
    dq_ref,
    dk_ref,
    dv_ref,
    q_s,
    do_s,
    km_ref,
    vm_ref,
    ke_ref,
    ve_ref,
    reach_ref,
    kv,
    bias,
    s_buf,
    dp_buf,
    p_s,
    ds_s,
    own,
    gsend,
    grecv,
    fsend,
    frecv,
    part,
    in_sem,
    q_sem,
    do_sem,
    a_send,
    a_recv,
    b_send,
    b_recv,
    d_send,
    d_recv,
    f_send,
    f_recv,
):
    rows = q_s.shape[1]
    length = km_ref.shape[2]
    width = q_s.shape[2]
    mine = km_ref.shape[3] // D
    heads = 2 * mine
    factor = D**-0.5

    h = lax.axis_index("head")
    r = lax.axis_index("inner")
    other = 1 - h
    has_prev = r > 0
    has_next = r < ring - 1

    def columns(slot):
        return pl.ds(pl.multiple_of(lax.rem(mine * h + slot, heads) * width, width), width)

    def load_q(slot):
        return pltpu.make_async_copy(q_hbm.at[0, 0, :, columns(slot)], q_s.at[slot], q_sem.at[slot])

    def load_do(slot):
        return pltpu.make_async_copy(
            do_hbm.at[0, 0, :, columns(slot)], do_s.at[slot], do_sem.at[slot]
        )

    def copy_a(j):
        return pltpu.make_async_remote_copy(
            src_ref=kv.at[j, :, pl.ds(length, length)],
            dst_ref=kv.at[mine + j, :, pl.ds(length, length)],
            send_sem=a_send.at[j],
            recv_sem=a_recv.at[j],
            device_id={"head": other},
            device_id_type=MESH,
        )

    def copy_b(slot):
        return pltpu.make_async_remote_copy(
            src_ref=kv.at[slot, :, pl.ds(length, length)],
            dst_ref=kv.at[slot, :, pl.ds(0, length)],
            send_sem=b_send.at[slot],
            recv_sem=b_recv.at[slot],
            device_id={"inner": r + 1},
            device_id_type=MESH,
        )

    def copy_d(slot):
        return pltpu.make_async_remote_copy(
            src_ref=gsend.at[slot],
            dst_ref=grecv.at[slot],
            send_sem=d_send.at[slot],
            recv_sem=d_recv.at[slot],
            device_id={"inner": r - 1},
            device_id_type=MESH,
        )

    def copy_f(j):
        return pltpu.make_async_remote_copy(
            src_ref=fsend.at[j],
            dst_ref=frecv.at[j],
            send_sem=f_send.at[j],
            recv_sem=f_recv.at[j],
            device_id={"head": other},
            device_id_type=MESH,
        )

    barrier = pltpu.get_barrier_semaphore()
    pl.semaphore_signal(barrier, inc=1, device_id={"head": other}, device_id_type=MESH)

    @pl.when(has_prev)
    def _():
        pl.semaphore_signal(barrier, inc=1, device_id={"inner": r - 1}, device_id_type=MESH)

    @pl.when(has_next)
    def _():
        pl.semaphore_signal(barrier, inc=1, device_id={"inner": r + 1}, device_id_type=MESH)

    small = [
        pltpu.make_async_copy(source, target, in_sem.at[n])
        for n, (source, target) in enumerate(
            (
                (ke_hbm, ke_ref),
                (ve_hbm, ve_ref),
                (km_hbm, km_ref),
                (vm_hbm, vm_ref),
                (reach_hbm, reach_ref),
            )
        )
    ]
    for copy in small:
        copy.start()
    for slot in range(heads):
        load_q(slot).start()
        load_do(slot).start()
    for copy in small:
        copy.wait()

    half = length // 2
    for j in range(mine):
        for b in range(2):
            for which, mant, exps in ((0, km_ref, ke_ref), (1, vm_ref, ve_ref)):
                block = mant[0, 0, b * half : (b + 1) * half, j * D : (j + 1) * D].astype(F32)
                kv[j, which, length + b * half : length + (b + 1) * half, :] = (
                    block * scale_of(exps[0, 0, b, j])
                ).astype(BF16)

    pl.semaphore_wait(barrier, 1 + has_prev.astype(jnp.int32) + has_next.astype(jnp.int32))

    for j in range(mine):

        @pl.when(has_next)
        def _():
            copy_b(j).start()

        copy_a(j).start()

    key_at = lax.broadcasted_iota(jnp.int32, (length, 2 * rows), 0)
    query_at = lax.rem(lax.broadcasted_iota(jnp.int32, (length, 2 * rows), 1), rows) + h * rows
    first_seen = jnp.where(has_prev, length - reach_ref[0, 0], length)
    bias[0:length, :] = jnp.where(key_at >= first_seen, 0.0, NEG_FILL).astype(F32)
    bias[length : 2 * length, :] = jnp.where(key_at <= query_at, 0.0, NEG_FILL).astype(F32)

    @pl.when(jnp.logical_not(has_prev))
    def _():
        for slot in range(heads):
            kv[slot, :, 0:length, :] = jnp.zeros((2, length, D), BF16)

    @pl.when(jnp.logical_not(has_next))
    def _():
        grecv[...] = jnp.zeros_like(grecv)

    def pass_on(j):
        copy_a(j).wait_recv()

        @pl.when(has_next)
        def _():
            copy_b(mine + j).start()

    def finish(j):
        @pl.when(has_next)
        def _():
            copy_d(mine + j).wait_recv()

        fsend[j] = (own[mine + j] + grecv[mine + j].astype(F32)).astype(BF16)
        copy_f(j).start()

    chunk = 64
    chunks = 2 * length // chunk
    wide = 2 * rows
    contract = (((1,), (1,)), ((), ()))

    def fold(x, op):
        folded = x[0:8]
        for at in range(8, chunk, 8):
            folded = op(folded, x[at : at + 8])
        return folded

    def softmax(pair):
        here = pair % 2
        span = slice(pair * wide, (pair + 1) * wide)
        peak = None
        for c in range(chunks):
            at = slice(c * chunk, (c + 1) * chunk)
            x = s_buf[here, at] * (factor * LOG2E) + bias[at]
            s_buf[here, at] = x
            top = fold(x, jnp.maximum)
            peak = top if peak is None else jnp.maximum(peak, top)
        peak = jnp.max(peak, axis=0, keepdims=True)
        total = None
        for c in range(chunks):
            at = slice(c * chunk, (c + 1) * chunk)
            x = jnp.exp2(s_buf[here, at] - peak)
            s_buf[here, at] = x
            some = fold(x, jnp.add)
            total = some if total is None else total + some
        inverse = 1.0 / jnp.sum(total, axis=0, keepdims=True)
        row_dot = None
        for c in range(chunks):
            at = slice(c * chunk, (c + 1) * chunk)
            rounded = (s_buf[here, at] * inverse).astype(BF16)
            p_s[at, span] = rounded
            some = fold(rounded.astype(F32) * dp_buf[here, at], jnp.add)
            row_dot = some if row_dot is None else row_dot + some
        row_dot = jnp.sum(row_dot, axis=0, keepdims=True)
        for c in range(chunks):
            at = slice(c * chunk, (c + 1) * chunk)
            x = (s_buf[here, at] * inverse) * (dp_buf[here, at] - row_dot)
            ds_s[at, span] = x.astype(BF16)

    def one_step(step, carry):
        slot = step + (step + heads - 2) // (heads - 1) - (heads - 1) * (step // (heads - 1))
        load_q(slot).wait()
        load_do(slot).wait()

        @pl.when(step == 1)
        def _():
            pass_on(1)

        @pl.when(has_prev)
        def _():
            copy_b(slot).wait_recv()

        q_list, do_list = [], []
        for pair in range(GROUP // 2):
            at = pair * 2 * D
            q_list.append(
                jnp.concatenate(
                    [q_s[slot, :, at : at + D], q_s[slot, :, at + D : at + 2 * D]], axis=0
                )
            )
            do_list.append(
                jnp.concatenate(
                    [do_s[slot, :, at : at + D], do_s[slot, :, at + D : at + 2 * D]], axis=0
                )
            )

        def first_products(pair):
            s_buf[pair % 2] = lax.dot_general(
                kv[slot, 0], q_list[pair], contract, preferred_element_type=F32
            )
            dp_buf[pair % 2] = lax.dot_general(
                kv[slot, 1], do_list[pair], contract, preferred_element_type=F32
            )

        def query_product(pair, keys_t):
            span = slice(pair * wide, (pair + 1) * wide)
            grad_t = jnp.dot(keys_t, ds_s[:, span], preferred_element_type=F32) * factor
            grad = grad_t.astype(BF16).T
            base = pl.multiple_of(lax.rem(mine * h + slot, heads) * width, width)
            for n in range(2):
                dq_ref[0, 0, :, pl.ds(base + (2 * pair + n) * D, D)] = grad[
                    n * rows : (n + 1) * rows
                ]

        def term_products(one, two):
            span = slice(one * wide, two * wide)
            dk = jnp.dot(
                ds_s[:, span],
                jnp.concatenate(q_list[one:two], axis=0),
                preferred_element_type=F32,
            )
            dv = jnp.dot(
                p_s[:, span],
                jnp.concatenate(do_list[one:two], axis=0),
                preferred_element_type=F32,
            )
            return dk * factor, dv

        keys_t = kv[slot, 0].T
        first_products(0)
        first_products(1)
        softmax(0)
        query_product(0, keys_t)
        first_products(2)
        softmax(1)
        query_product(1, keys_t)
        first_products(3)
        dk, dv = term_products(0, 2)
        own[slot, 0] = dk[length:]
        own[slot, 1] = dv[length:]
        part[0] = dk[:length]
        part[1] = dv[:length]
        softmax(2)
        query_product(2, keys_t)

        @pl.when(step == 0)
        def _():
            pass_on(0)

        @pl.when(step == heads - 1)
        def _():
            finish(1)

        softmax(3)
        query_product(3, keys_t)
        dk, dv = term_products(2, 4)
        gsend[slot, 0] = (part[0] + dk[:length]).astype(BF16)
        gsend[slot, 1] = (part[1] + dv[:length]).astype(BF16)

        @pl.when(has_prev)
        def _():
            copy_d(slot).start()

        own[slot, 0] += dk[length:]
        own[slot, 1] += dv[length:]

        @pl.when(step == heads - 2)
        def _():
            finish(0)

        return carry

    lax.fori_loop(0, heads, one_step, 0)

    for j in range(mine):

        @pl.when(has_next)
        def _():
            copy_d(j).wait_recv()

        copy_f(j).wait_recv()
        total = own[j] + grecv[j].astype(F32) + frecv[j].astype(F32)
        dk_ref[0, 0, :, j * D : (j + 1) * D] = total[0].astype(BF16)
        dv_ref[0, 0, :, j * D : (j + 1) * D] = total[1].astype(BF16)

    for j in range(mine):
        copy_a(j).wait_send()
        copy_f(j).wait_send()
    for slot in range(heads):

        @pl.when(has_next)
        def _():
            copy_b(slot).wait_send()

        @pl.when(has_prev)
        def _():
            copy_d(slot).wait_send()


def hand_over(dq_ref, dk_ref, dv_ref, dq_hbm, dk_hbm, dv_hbm, sem):
    rows = dq_ref.shape[2]
    copies = [
        pltpu.make_async_copy(dk_ref, dk_hbm, sem.at[0]),
        pltpu.make_async_copy(dv_ref, dv_hbm, sem.at[1]),
    ]
    for n in range(4):
        at = pl.ds(n * (rows // 4), rows // 4)
        copies.append(
            pltpu.make_async_copy(dq_ref.at[:, :, at], dq_hbm.at[:, :, at], sem.at[2 + n])
        )
    for copy in copies:
        copy.start()
    for copy in copies:
        copy.wait()


def on_device(ring, query, dout, key_mant, value_mantissas, key_exps, value_exponents, reach):
    rows, length = query.shape[2], key_mant.shape[2]
    mine = key_mant.shape[3] // D
    heads = 2 * mine
    width = GROUP * D
    hbm = pl.BlockSpec(memory_space=pltpu.HBM)
    vmem = pl.BlockSpec(memory_space=pltpu.VMEM)
    dma = pltpu.SemaphoreType.DMA
    out_shape = (
        jax.ShapeDtypeStruct(query.shape, BF16),
        jax.ShapeDtypeStruct(key_mant.shape, BF16),
        jax.ShapeDtypeStruct(key_mant.shape, BF16),
    )
    grads = pl.pallas_call(
        functools.partial(kernel, ring),
        out_shape=out_shape,
        in_specs=[hbm] * 7,
        out_specs=(vmem, vmem, vmem),
        scratch_shapes=[
            pltpu.VMEM((heads, rows, width), BF16),
            pltpu.VMEM((heads, rows, width), BF16),
            pltpu.VMEM(key_mant.shape, BF16),
            pltpu.VMEM(key_mant.shape, BF16),
            pltpu.SMEM(key_exps.shape, jnp.int32),
            pltpu.SMEM(key_exps.shape, jnp.int32),
            pltpu.SMEM(reach.shape, jnp.int32),
            pltpu.VMEM((heads, 2, 2 * length, D), BF16),
            pltpu.VMEM((2 * length, 2 * rows), F32),
            pltpu.VMEM((2, 2 * length, 2 * rows), F32),
            pltpu.VMEM((2, 2 * length, 2 * rows), F32),
            pltpu.VMEM((2 * length, GROUP * rows), BF16),
            pltpu.VMEM((2 * length, GROUP * rows), BF16),
            pltpu.VMEM((heads, 2, length, D), F32),
            pltpu.VMEM((heads, 2, length, D), BF16),
            pltpu.VMEM((heads, 2, length, D), BF16),
            pltpu.VMEM((mine, 2, length, D), BF16),
            pltpu.VMEM((mine, 2, length, D), BF16),
            pltpu.VMEM((2, length, D), F32),
            dma((5,)),
            dma((heads,)),
            dma((heads,)),
            dma((mine,)),
            dma((mine,)),
            dma((heads,)),
            dma((heads,)),
            dma((heads,)),
            dma((heads,)),
            dma((mine,)),
            dma((mine,)),
        ],
        compiler_params=pltpu.CompilerParams(
            collective_id=0, has_side_effects=True, vmem_limit_bytes=48 * 2**20
        ),
        cost_estimate=pl.CostEstimate(
            flops=10 * heads * width * rows * 2 * length,
            bytes_accessed=6 * rows * heads * width,
            transcendentals=heads * GROUP * rows * 2 * length,
        ),
    )(query, dout, key_mant, value_mantissas, key_exps, value_exponents, reach)
    return pl.pallas_call(
        hand_over,
        out_shape=out_shape,
        in_specs=[vmem] * 3,
        out_specs=(hbm, hbm, hbm),
        scratch_shapes=[dma((6,))],
    )(*grads)


def solution(mesh):
    assert mesh.shape["head"] == 2
    tokens = P("outer", "inner", "head", None)
    shared = P("outer", "inner", None, "head")
    return jax.shard_map(
        functools.partial(on_device, mesh.shape["inner"]),
        mesh=mesh,
        in_specs=(tokens, tokens, shared, shared, shared, shared, P("outer", "inner")),
        out_specs=(tokens, shared, shared),
        check_vma=False,
    )
```

```python
import functools

import jax
import jax.numpy as jnp
from jax import lax
from jax.experimental import pallas as pl
from jax.experimental.pallas import tpu as pltpu
from jax.sharding import PartitionSpec as P

D = 128
GROUP = 8
LOG2E = 1.4426950408889634
NEG_FILL = -1e30
F32 = jnp.float32
BF16 = jnp.bfloat16
MESH = pl.DeviceIdType.MESH


def scale_of(exponent):
    return jnp.where(exponent > 0, 2.0, jnp.where(exponent < 0, 0.5, 1.0)).astype(F32)


def kernel(
    ring,
    q_hbm,
    do_hbm,
    km_hbm,
    vm_hbm,
    ke_hbm,
    ve_hbm,
    reach_hbm,
    dq_hbm,
    dk_ref,
    dv_ref,
    q_s,
    do_s,
    dq_s,
    km_ref,
    vm_ref,
    ke_ref,
    ve_ref,
    reach_ref,
    kv,
    bias,
    s_buf,
    p_s,
    ds_s,
    own,
    gsend,
    grecv,
    fsend,
    frecv,
    part,
    in_sem,
    q_sem,
    do_sem,
    dq_sem,
    a_send,
    a_recv,
    b_send,
    b_recv,
    d_send,
    d_recv,
    f_send,
    f_recv,
):
    rows = q_s.shape[1]
    length = km_ref.shape[2]
    width = q_s.shape[2]
    mine = km_ref.shape[3] // D
    heads = 2 * mine
    factor = D**-0.5

    h = lax.axis_index("head")
    r = lax.axis_index("inner")
    other = 1 - h
    has_prev = r > 0
    has_next = r < ring - 1

    def columns(slot):
        return pl.ds(pl.multiple_of(lax.rem(mine * h + slot, heads) * width, width), width)

    def load_q(slot):
        return pltpu.make_async_copy(q_hbm.at[0, 0, :, columns(slot)], q_s.at[slot], q_sem.at[slot])

    def load_do(slot):
        return pltpu.make_async_copy(
            do_hbm.at[0, 0, :, columns(slot)], do_s.at[slot], do_sem.at[slot]
        )

    def store_dq(slot):
        return pltpu.make_async_copy(
            dq_s.at[slot], dq_hbm.at[0, 0, :, columns(slot)], dq_sem.at[slot]
        )

    def copy_a(j):
        return pltpu.make_async_remote_copy(
            src_ref=kv.at[j, :, pl.ds(length, length)],
            dst_ref=kv.at[mine + j, :, pl.ds(length, length)],
            send_sem=a_send.at[j],
            recv_sem=a_recv.at[j],
            device_id={"head": other},
            device_id_type=MESH,
        )

    def copy_b(slot):
        return pltpu.make_async_remote_copy(
            src_ref=kv.at[slot, :, pl.ds(length, length)],
            dst_ref=kv.at[slot, :, pl.ds(0, length)],
            send_sem=b_send.at[slot],
            recv_sem=b_recv.at[slot],
            device_id={"inner": r + 1},
            device_id_type=MESH,
        )

    def copy_d(slot):
        return pltpu.make_async_remote_copy(
            src_ref=gsend.at[slot],
            dst_ref=grecv.at[slot],
            send_sem=d_send.at[slot],
            recv_sem=d_recv.at[slot],
            device_id={"inner": r - 1},
            device_id_type=MESH,
        )

    def copy_f(j):
        return pltpu.make_async_remote_copy(
            src_ref=fsend.at[j],
            dst_ref=frecv.at[j],
            send_sem=f_send.at[j],
            recv_sem=f_recv.at[j],
            device_id={"head": other},
            device_id_type=MESH,
        )

    barrier = pltpu.get_barrier_semaphore()
    pl.semaphore_signal(barrier, inc=1, device_id={"head": other}, device_id_type=MESH)

    @pl.when(has_prev)
    def _():
        pl.semaphore_signal(barrier, inc=1, device_id={"inner": r - 1}, device_id_type=MESH)

    @pl.when(has_next)
    def _():
        pl.semaphore_signal(barrier, inc=1, device_id={"inner": r + 1}, device_id_type=MESH)

    small = [
        pltpu.make_async_copy(source, target, in_sem.at[n])
        for n, (source, target) in enumerate(
            (
                (ke_hbm, ke_ref),
                (ve_hbm, ve_ref),
                (km_hbm, km_ref),
                (vm_hbm, vm_ref),
                (reach_hbm, reach_ref),
            )
        )
    ]
    for copy in small:
        copy.start()
    for slot in range(heads):
        load_q(slot).start()
        load_do(slot).start()
    for copy in small:
        copy.wait()

    half = length // 2
    for j in range(mine):
        for b in range(2):
            for which, mant, exps in ((0, km_ref, ke_ref), (1, vm_ref, ve_ref)):
                block = mant[0, 0, b * half : (b + 1) * half, j * D : (j + 1) * D].astype(F32)
                kv[j, which, length + b * half : length + (b + 1) * half, :] = (
                    block * scale_of(exps[0, 0, b, j])
                ).astype(BF16)

    pl.semaphore_wait(barrier, 1 + has_prev.astype(jnp.int32) + has_next.astype(jnp.int32))

    for j in range(mine):

        @pl.when(has_next)
        def _():
            copy_b(j).start()

        copy_a(j).start()

    key_at = lax.broadcasted_iota(jnp.int32, (length, 2 * rows), 0)
    query_at = lax.rem(lax.broadcasted_iota(jnp.int32, (length, 2 * rows), 1), rows) + h * rows
    first_seen = jnp.where(has_prev, length - reach_ref[0, 0], length)
    bias[0:length, :] = jnp.where(key_at >= first_seen, 0.0, NEG_FILL).astype(F32)
    bias[length : 2 * length, :] = jnp.where(key_at <= query_at, 0.0, NEG_FILL).astype(F32)

    @pl.when(jnp.logical_not(has_prev))
    def _():
        for slot in range(heads):
            kv[slot, :, 0:length, :] = jnp.zeros((2, length, D), BF16)

    @pl.when(jnp.logical_not(has_next))
    def _():
        grecv[...] = jnp.zeros_like(grecv)

    def pass_on(j):
        copy_a(j).wait_recv()

        @pl.when(has_next)
        def _():
            copy_b(mine + j).start()

    def finish(j):
        @pl.when(has_next)
        def _():
            copy_d(mine + j).wait_recv()

        fsend[j] = (own[mine + j] + grecv[mine + j].astype(F32)).astype(BF16)
        copy_f(j).start()

    chunk = 64
    chunks = 2 * length // chunk
    wide = 2 * rows
    contract = (((1,), (1,)), ((), ()))

    def fold(x, op):
        folded = x[0:8]
        for at in range(8, x.shape[0], 8):
            folded = op(folded, x[at : at + 8])
        return folded

    def one_step(step, carry):
        slot = step + (step + heads - 2) // (heads - 1) - (heads - 1) * (step // (heads - 1))
        load_q(slot).wait()
        load_do(slot).wait()

        @pl.when(step == 1)
        def _():
            pass_on(1)

        @pl.when(has_prev)
        def _():
            copy_b(slot).wait_recv()

        keys_t = kv[slot, 0].T
        values_t = kv[slot, 1].T
        q_list, do_list = [], []
        for pair in range(GROUP // 2):
            at = pair * 2 * D
            q_list.append(
                jnp.concatenate(
                    [q_s[slot, :, at : at + D], q_s[slot, :, at + D : at + 2 * D]], axis=0
                )
            )
            do_list.append(
                jnp.concatenate(
                    [do_s[slot, :, at : at + D], do_s[slot, :, at + D : at + 2 * D]], axis=0
                )
            )

        def scores(pair):
            x = lax.dot_general(kv[slot, 0], q_list[pair], contract, preferred_element_type=F32)
            x = x * (factor * LOG2E) + bias[...]
            s_buf[pair % 2] = x
            return jnp.max(fold(x, jnp.maximum), axis=0, keepdims=True)

        def softmax(pair, peak):
            here = pair % 2
            span = slice(pair * wide, (pair + 1) * wide)
            total = None
            for c in range(chunks):
                at = slice(c * chunk, (c + 1) * chunk)
                x = jnp.exp2(s_buf[here, at] - peak)
                s_buf[here, at] = x
                some = fold(x, jnp.add)
                total = some if total is None else total + some
            inverse = 1.0 / jnp.sum(total, axis=0, keepdims=True)
            for c in range(chunks):
                at = slice(c * chunk, (c + 1) * chunk)
                p_s[at, span] = (s_buf[here, at] * inverse).astype(BF16)
            return inverse

        def score_grads(pair, inverse):
            here = pair % 2
            span = slice(pair * wide, (pair + 1) * wide)
            do_t = do_list[pair].T
            output_t = jnp.dot(values_t, p_s[:, span], preferred_element_type=F32)
            row_dot = jnp.sum(fold(do_t.astype(F32) * output_t, jnp.add), axis=0, keepdims=True)
            dprob = jnp.dot(kv[slot, 1], do_t, preferred_element_type=F32)
            ds_s[:, span] = ((s_buf[here] * inverse) * (dprob - row_dot)).astype(BF16)

        def query_product(pair):
            span = slice(pair * wide, (pair + 1) * wide)
            grad_t = jnp.dot(keys_t, ds_s[:, span], preferred_element_type=F32) * factor
            grad = grad_t.astype(BF16).T
            for n in range(2):
                at = (2 * pair + n) * D
                dq_s[slot, :, at : at + D] = grad[n * rows : (n + 1) * rows]

        def term_products(one, two):
            span = slice(one * wide, two * wide)
            dk = jnp.dot(
                ds_s[:, span],
                jnp.concatenate(q_list[one:two], axis=0),
                preferred_element_type=F32,
            )
            dv = jnp.dot(
                p_s[:, span],
                jnp.concatenate(do_list[one:two], axis=0),
                preferred_element_type=F32,
            )
            return dk * factor, dv

        peak = scores(0)
        inverse = softmax(0, peak)
        peak = scores(1)
        score_grads(0, inverse)
        inverse = softmax(1, peak)
        query_product(0)
        peak = scores(2)
        score_grads(1, inverse)
        inverse = softmax(2, peak)
        query_product(1)
        dk, dv = term_products(0, 2)
        own[slot, 0] = dk[length:]
        own[slot, 1] = dv[length:]
        part[0] = dk[:length]
        part[1] = dv[:length]
        peak = scores(3)
        score_grads(2, inverse)

        @pl.when(step == 0)
        def _():
            pass_on(0)

        @pl.when(step == heads - 1)
        def _():
            finish(1)

        inverse = softmax(3, peak)
        query_product(2)
        score_grads(3, inverse)
        query_product(3)
        store_dq(slot).start()
        dk, dv = term_products(2, 4)
        gsend[slot, 0] = (part[0] + dk[:length]).astype(BF16)
        gsend[slot, 1] = (part[1] + dv[:length]).astype(BF16)

        @pl.when(has_prev)
        def _():
            copy_d(slot).start()

        own[slot, 0] += dk[length:]
        own[slot, 1] += dv[length:]

        @pl.when(step == heads - 2)
        def _():
            finish(0)

        return carry

    lax.fori_loop(0, heads, one_step, 0)

    for j in range(mine):

        @pl.when(has_next)
        def _():
            copy_d(j).wait_recv()

        copy_f(j).wait_recv()
        total = own[j] + grecv[j].astype(F32) + frecv[j].astype(F32)
        dk_ref[0, 0, :, j * D : (j + 1) * D] = total[0].astype(BF16)
        dv_ref[0, 0, :, j * D : (j + 1) * D] = total[1].astype(BF16)

    for j in range(mine):
        copy_a(j).wait_send()
        copy_f(j).wait_send()
    for slot in range(heads):
        store_dq(slot).wait()

        @pl.when(has_next)
        def _():
            copy_b(slot).wait_send()

        @pl.when(has_prev)
        def _():
            copy_d(slot).wait_send()


def on_device(ring, query, dout, key_mant, value_mantissas, key_exps, value_exponents, reach):
    rows, length = query.shape[2], key_mant.shape[2]
    mine = key_mant.shape[3] // D
    heads = 2 * mine
    width = GROUP * D
    hbm = pl.BlockSpec(memory_space=pltpu.HBM)
    vmem = pl.BlockSpec(memory_space=pltpu.VMEM)
    dma = pltpu.SemaphoreType.DMA
    out_shape = (
        jax.ShapeDtypeStruct(query.shape, BF16),
        jax.ShapeDtypeStruct(key_mant.shape, BF16),
        jax.ShapeDtypeStruct(key_mant.shape, BF16),
    )
    return pl.pallas_call(
        functools.partial(kernel, ring),
        out_shape=out_shape,
        in_specs=[hbm] * 7,
        out_specs=(hbm, vmem, vmem),
        scratch_shapes=[
            pltpu.VMEM((heads, rows, width), BF16),
            pltpu.VMEM((heads, rows, width), BF16),
            pltpu.VMEM((heads, rows, width), BF16),
            pltpu.VMEM(key_mant.shape, BF16),
            pltpu.VMEM(key_mant.shape, BF16),
            pltpu.SMEM(key_exps.shape, jnp.int32),
            pltpu.SMEM(key_exps.shape, jnp.int32),
            pltpu.SMEM(reach.shape, jnp.int32),
            pltpu.VMEM((heads, 2, 2 * length, D), BF16),
            pltpu.VMEM((2 * length, 2 * rows), F32),
            pltpu.VMEM((2, 2 * length, 2 * rows), F32),
            pltpu.VMEM((2 * length, GROUP * rows), BF16),
            pltpu.VMEM((2 * length, GROUP * rows), BF16),
            pltpu.VMEM((heads, 2, length, D), F32),
            pltpu.VMEM((heads, 2, length, D), BF16),
            pltpu.VMEM((heads, 2, length, D), BF16),
            pltpu.VMEM((mine, 2, length, D), BF16),
            pltpu.VMEM((mine, 2, length, D), BF16),
            pltpu.VMEM((2, length, D), F32),
            dma((5,)),
            dma((heads,)),
            dma((heads,)),
            dma((heads,)),
            dma((mine,)),
            dma((mine,)),
            dma((heads,)),
            dma((heads,)),
            dma((heads,)),
            dma((heads,)),
            dma((mine,)),
            dma((mine,)),
        ],
        compiler_params=pltpu.CompilerParams(
            collective_id=0, has_side_effects=True, vmem_limit_bytes=60 * 2**20
        ),
        cost_estimate=pl.CostEstimate(
            flops=10 * heads * width * rows * 2 * length,
            bytes_accessed=6 * rows * heads * width,
            transcendentals=heads * GROUP * rows * 2 * length,
        ),
    )(query, dout, key_mant, value_mantissas, key_exps, value_exponents, reach)

def solution(mesh):
    assert mesh.shape["head"] == 2
    tokens = P("outer", "inner", "head", None)
    shared = P("outer", "inner", None, "head")
    return jax.shard_map(
        functools.partial(on_device, mesh.shape["inner"]),
        mesh=mesh,
        in_specs=(tokens, tokens, shared, shared, shared, shared, P("outer", "inner")),
        out_specs=(tokens, shared, shared),
        check_vma=False,
    )
```

```python
import functools

import jax
import jax.numpy as jnp
from jax import lax
from jax.experimental import pallas as pl
from jax.experimental.pallas import tpu as pltpu
from jax.sharding import PartitionSpec as P

D = 128
GROUP = 8
LOG2E = 1.4426950408889634
NEG_FILL = -1e30
F32 = jnp.float32
BF16 = jnp.bfloat16
MESH = pl.DeviceIdType.MESH


def scale_of(exponent):
    return jnp.where(exponent > 0, 2.0, jnp.where(exponent < 0, 0.5, 1.0)).astype(F32)


def kernel(
    ring,
    q_hbm,
    do_hbm,
    km_hbm,
    vm_hbm,
    ke_hbm,
    ve_hbm,
    reach_hbm,
    dq_ref,
    dk_ref,
    dv_ref,
    q_s,
    do_s,
    km_ref,
    vm_ref,
    ke_ref,
    ve_ref,
    reach_ref,
    kv,
    bias,
    s_buf,
    p_s,
    ds_s,
    own,
    gsend,
    grecv,
    fsend,
    frecv,
    in_sem,
    q_sem,
    do_sem,
    a_send,
    a_recv,
    b_send,
    b_recv,
    d_send,
    d_recv,
    f_send,
    f_recv,
):
    rows = q_s.shape[1]
    length = km_ref.shape[2]
    width = q_s.shape[2]
    mine = km_ref.shape[3] // D
    heads = 2 * mine
    factor = D**-0.5

    h = lax.axis_index("head")
    r = lax.axis_index("inner")
    other = 1 - h
    has_prev = r > 0
    has_next = r < ring - 1

    def columns(slot):
        return pl.ds(pl.multiple_of(lax.rem(mine * h + slot, heads) * width, width), width)

    def load_q(slot):
        return pltpu.make_async_copy(q_hbm.at[0, 0, :, columns(slot)], q_s.at[slot], q_sem.at[slot])

    def load_do(slot):
        return pltpu.make_async_copy(
            do_hbm.at[0, 0, :, columns(slot)], do_s.at[slot], do_sem.at[slot]
        )

    def copy_a(j):
        return pltpu.make_async_remote_copy(
            src_ref=kv.at[j, :, pl.ds(length, length)],
            dst_ref=kv.at[mine + j, :, pl.ds(length, length)],
            send_sem=a_send.at[j],
            recv_sem=a_recv.at[j],
            device_id={"head": other},
            device_id_type=MESH,
        )

    def copy_b(slot):
        return pltpu.make_async_remote_copy(
            src_ref=kv.at[slot, :, pl.ds(length, length)],
            dst_ref=kv.at[slot, :, pl.ds(0, length)],
            send_sem=b_send.at[slot],
            recv_sem=b_recv.at[slot],
            device_id={"inner": r + 1},
            device_id_type=MESH,
        )

    def copy_d(slot):
        return pltpu.make_async_remote_copy(
            src_ref=gsend.at[slot],
            dst_ref=grecv.at[slot],
            send_sem=d_send.at[slot],
            recv_sem=d_recv.at[slot],
            device_id={"inner": r - 1},
            device_id_type=MESH,
        )

    def copy_f(j):
        return pltpu.make_async_remote_copy(
            src_ref=fsend.at[j],
            dst_ref=frecv.at[j],
            send_sem=f_send.at[j],
            recv_sem=f_recv.at[j],
            device_id={"head": other},
            device_id_type=MESH,
        )

    barrier = pltpu.get_barrier_semaphore()
    pl.semaphore_signal(barrier, inc=1, device_id={"head": other}, device_id_type=MESH)

    @pl.when(has_prev)
    def _():
        pl.semaphore_signal(barrier, inc=1, device_id={"inner": r - 1}, device_id_type=MESH)

    @pl.when(has_next)
    def _():
        pl.semaphore_signal(barrier, inc=1, device_id={"inner": r + 1}, device_id_type=MESH)

    small = [
        pltpu.make_async_copy(source, target, in_sem.at[n])
        for n, (source, target) in enumerate(
            (
                (ke_hbm, ke_ref),
                (ve_hbm, ve_ref),
                (km_hbm, km_ref),
                (vm_hbm, vm_ref),
                (reach_hbm, reach_ref),
            )
        )
    ]
    for copy in small:
        copy.start()
    for slot in range(heads):
        load_q(slot).start()
        load_do(slot).start()
    for copy in small:
        copy.wait()

    half = length // 2
    for j in range(mine):
        for b in range(2):
            for which, mant, exps in ((0, km_ref, ke_ref), (1, vm_ref, ve_ref)):
                block = mant[0, 0, b * half : (b + 1) * half, j * D : (j + 1) * D].astype(F32)
                kv[j, which, length + b * half : length + (b + 1) * half, :] = (
                    block * scale_of(exps[0, 0, b, j])
                ).astype(BF16)

    pl.semaphore_wait(barrier, 1 + has_prev.astype(jnp.int32) + has_next.astype(jnp.int32))

    for j in range(mine):

        @pl.when(has_next)
        def _():
            copy_b(j).start()

        copy_a(j).start()

    key_at = lax.broadcasted_iota(jnp.int32, (length, 2 * rows), 0)
    query_at = lax.rem(lax.broadcasted_iota(jnp.int32, (length, 2 * rows), 1), rows) + h * rows
    first_seen = jnp.where(has_prev, length - reach_ref[0, 0], length)
    bias[0:length, :] = jnp.where(key_at >= first_seen, 0.0, NEG_FILL).astype(F32)
    bias[length : 2 * length, :] = jnp.where(key_at <= query_at, 0.0, NEG_FILL).astype(F32)

    @pl.when(jnp.logical_not(has_prev))
    def _():
        for slot in range(heads):
            kv[slot, :, 0:length, :] = jnp.zeros((2, length, D), BF16)

    @pl.when(jnp.logical_not(has_next))
    def _():
        grecv[...] = jnp.zeros_like(grecv)

    def pass_on(j):
        copy_a(j).wait_recv()

        @pl.when(has_next)
        def _():
            copy_b(mine + j).start()

    def finish(j):
        @pl.when(has_next)
        def _():
            copy_d(mine + j).wait_recv()

        fsend[j] = (own[mine + j] + grecv[mine + j].astype(F32)).astype(BF16)
        copy_f(j).start()

    chunk = 64
    chunks = 2 * length // chunk
    wide = 2 * rows
    pairs = GROUP // 2
    contract = (((1,), (1,)), ((), ()))

    def fold(x, op):
        folded = x[0:8]
        for at in range(8, x.shape[0], 8):
            folded = op(folded, x[at : at + 8])
        return folded

    def one_step(step, carry):
        slot = step + (step + heads - 2) // (heads - 1) - (heads - 1) * (step // (heads - 1))
        load_q(slot).wait()
        load_do(slot).wait()

        @pl.when(step == 1)
        def _():
            pass_on(1)

        @pl.when(has_prev)
        def _():
            copy_b(slot).wait_recv()

        keys_t = kv[slot, 0].T
        values_t = kv[slot, 1].T
        def stacked(ref):
            return jnp.concatenate(
                [ref[slot, :, n * D : (n + 1) * D] for n in range(GROUP)], axis=0
            )

        q_all = stacked(q_s)
        do_all = stacked(do_s)
        do_t = do_all.T
        x = lax.dot_general(kv[slot, 0], q_all, contract, preferred_element_type=F32)
        inverses = []
        for pair in range(pairs):
            span = slice(pair * wide, (pair + 1) * wide)
            some = x[:, span] * (factor * LOG2E) + bias[...]
            s_buf[:, span] = some
            peak = jnp.max(fold(some, jnp.maximum), axis=0, keepdims=True)
            total = None
            for c in range(chunks):
                at = slice(c * chunk, (c + 1) * chunk)
                weights = jnp.exp2(s_buf[at, span] - peak)
                s_buf[at, span] = weights
                some = fold(weights, jnp.add)
                total = some if total is None else total + some
            inverse = 1.0 / jnp.sum(total, axis=0, keepdims=True)
            inverses.append(inverse)
            for c in range(chunks):
                at = slice(c * chunk, (c + 1) * chunk)
                p_s[at, span] = (s_buf[at, span] * inverse).astype(BF16)

        @pl.when(step == 0)
        def _():
            pass_on(0)

        output_t = jnp.dot(values_t, p_s[...], preferred_element_type=F32)
        dprob = jnp.dot(kv[slot, 1], do_t, preferred_element_type=F32)
        dv = jnp.dot(p_s[...], do_all, preferred_element_type=F32)
        for pair in range(pairs):
            span = slice(pair * wide, (pair + 1) * wide)
            row_dot = jnp.sum(
                fold(do_t[:, span].astype(F32) * output_t[:, span], jnp.add),
                axis=0,
                keepdims=True,
            )
            ds_s[:, span] = (
                (s_buf[:, span] * inverses[pair]) * (dprob[:, span] - row_dot)
            ).astype(BF16)
        own[slot, 1] = dv[length:]
        gsend[slot, 1] = dv[:length].astype(BF16)

        @pl.when(step == heads - 1)
        def _():
            finish(1)

        dk = jnp.dot(ds_s[...], q_all, preferred_element_type=F32) * factor
        gsend[slot, 0] = dk[:length].astype(BF16)

        @pl.when(has_prev)
        def _():
            copy_d(slot).start()

        own[slot, 0] = dk[length:]
        grad_t = jnp.dot(keys_t, ds_s[...], preferred_element_type=F32) * factor
        grad = grad_t.astype(BF16).T
        base = pl.multiple_of(lax.rem(mine * h + slot, heads) * width, width)
        for n in range(GROUP):
            dq_ref[0, 0, :, pl.ds(base + n * D, D)] = grad[n * rows : (n + 1) * rows]

        @pl.when(step == heads - 2)
        def _():
            finish(0)

        return carry

    lax.fori_loop(0, heads, one_step, 0)

    for j in range(mine):

        @pl.when(has_next)
        def _():
            copy_d(j).wait_recv()

        copy_f(j).wait_recv()
        total = own[j] + grecv[j].astype(F32) + frecv[j].astype(F32)
        dk_ref[0, 0, :, j * D : (j + 1) * D] = total[0].astype(BF16)
        dv_ref[0, 0, :, j * D : (j + 1) * D] = total[1].astype(BF16)

    for j in range(mine):
        copy_a(j).wait_send()
        copy_f(j).wait_send()
    for slot in range(heads):
        @pl.when(has_next)
        def _():
            copy_b(slot).wait_send()

        @pl.when(has_prev)
        def _():
            copy_d(slot).wait_send()


def on_device(ring, query, dout, key_mant, value_mantissas, key_exps, value_exponents, reach):
    rows, length = query.shape[2], key_mant.shape[2]
    mine = key_mant.shape[3] // D
    heads = 2 * mine
    width = GROUP * D
    hbm = pl.BlockSpec(memory_space=pltpu.HBM)
    vmem = pl.BlockSpec(memory_space=pltpu.VMEM)
    dma = pltpu.SemaphoreType.DMA
    out_shape = (
        pltpu.VMEM(query.shape, BF16),
        pltpu.VMEM(key_mant.shape, BF16),
        pltpu.VMEM(key_mant.shape, BF16),
    )
    return pl.pallas_call(
        functools.partial(kernel, ring),
        out_shape=out_shape,
        in_specs=[hbm] * 7,
        out_specs=(vmem, vmem, vmem),
        scratch_shapes=[
            pltpu.VMEM((heads, rows, width), BF16),
            pltpu.VMEM((heads, rows, width), BF16),
            pltpu.VMEM(key_mant.shape, BF16),
            pltpu.VMEM(key_mant.shape, BF16),
            pltpu.SMEM(key_exps.shape, jnp.int32),
            pltpu.SMEM(key_exps.shape, jnp.int32),
            pltpu.SMEM(reach.shape, jnp.int32),
            pltpu.VMEM((heads, 2, 2 * length, D), BF16),
            pltpu.VMEM((2 * length, 2 * rows), F32),
            pltpu.VMEM((2 * length, GROUP * rows), F32),
            pltpu.VMEM((2 * length, GROUP * rows), BF16),
            pltpu.VMEM((2 * length, GROUP * rows), BF16),
            pltpu.VMEM((heads, 2, length, D), F32),
            pltpu.VMEM((heads, 2, length, D), BF16),
            pltpu.VMEM((heads, 2, length, D), BF16),
            pltpu.VMEM((mine, 2, length, D), BF16),
            pltpu.VMEM((mine, 2, length, D), BF16),
            dma((5,)),
            dma((heads,)),
            dma((heads,)),
            dma((mine,)),
            dma((mine,)),
            dma((heads,)),
            dma((heads,)),
            dma((heads,)),
            dma((heads,)),
            dma((mine,)),
            dma((mine,)),
        ],
        compiler_params=pltpu.CompilerParams(
            collective_id=0, has_side_effects=True, vmem_limit_bytes=56 * 2**20
        ),
        cost_estimate=pl.CostEstimate(
            flops=10 * heads * width * rows * 2 * length,
            bytes_accessed=6 * rows * heads * width,
            transcendentals=heads * GROUP * rows * 2 * length,
        ),
    )(query, dout, key_mant, value_mantissas, key_exps, value_exponents, reach)

def solution(mesh):
    assert mesh.shape["head"] == 2
    tokens = P("outer", "inner", "head", None)
    shared = P("outer", "inner", None, "head")
    return jax.shard_map(
        functools.partial(on_device, mesh.shape["inner"]),
        mesh=mesh,
        in_specs=(tokens, tokens, shared, shared, shared, shared, P("outer", "inner")),
        out_specs=(tokens, shared, shared),
        check_vma=False,
    )
```

```python
import functools

import jax
import jax.numpy as jnp
from jax import lax
from jax.experimental import pallas as pl
from jax.experimental.pallas import tpu as pltpu
from jax.sharding import PartitionSpec as P

D = 128
GROUP = 8
LOG2E = 1.4426950408889634
NEG_FILL = -1e30
F32 = jnp.float32
BF16 = jnp.bfloat16
MESH = pl.DeviceIdType.MESH


def scale_of(exponent):
    return jnp.where(exponent > 0, 2.0, jnp.where(exponent < 0, 0.5, 1.0)).astype(F32)


def kernel(
    ring,
    q_hbm,
    do_hbm,
    km_hbm,
    vm_hbm,
    ke_hbm,
    ve_hbm,
    reach_hbm,
    dq_ref,
    dk_ref,
    dv_ref,
    q_s,
    do_s,
    km_ref,
    vm_ref,
    ke_ref,
    ve_ref,
    reach_ref,
    kv,
    bias,
    q_st,
    do_st,
    s_buf,
    dp_buf,
    p_s,
    ds_s,
    own,
    gsend,
    grecv,
    fsend,
    frecv,
    in_sem,
    q_sem,
    do_sem,
    a_send,
    a_recv,
    b_send,
    b_recv,
    d_send,
    d_recv,
    f_send,
    f_recv,
):
    rows = q_s.shape[1]
    length = km_ref.shape[2]
    width = q_s.shape[2]
    mine = km_ref.shape[3] // D
    heads = 2 * mine
    factor = D**-0.5

    h = lax.axis_index("head")
    r = lax.axis_index("inner")
    other = 1 - h
    has_prev = r > 0
    has_next = r < ring - 1

    def columns(slot):
        return pl.ds(pl.multiple_of(lax.rem(mine * h + slot, heads) * width, width), width)

    def load_q(slot):
        return pltpu.make_async_copy(q_hbm.at[0, 0, :, columns(slot)], q_s.at[slot], q_sem.at[slot])

    def load_do(slot):
        return pltpu.make_async_copy(
            do_hbm.at[0, 0, :, columns(slot)], do_s.at[slot], do_sem.at[slot]
        )

    def copy_a(j):
        return pltpu.make_async_remote_copy(
            src_ref=kv.at[j, :, pl.ds(length, length)],
            dst_ref=kv.at[mine + j, :, pl.ds(length, length)],
            send_sem=a_send.at[j],
            recv_sem=a_recv.at[j],
            device_id={"head": other},
            device_id_type=MESH,
        )

    def copy_b(slot):
        return pltpu.make_async_remote_copy(
            src_ref=kv.at[slot, :, pl.ds(length, length)],
            dst_ref=kv.at[slot, :, pl.ds(0, length)],
            send_sem=b_send.at[slot],
            recv_sem=b_recv.at[slot],
            device_id={"inner": r + 1},
            device_id_type=MESH,
        )

    def copy_d(slot):
        return pltpu.make_async_remote_copy(
            src_ref=gsend.at[slot],
            dst_ref=grecv.at[slot],
            send_sem=d_send.at[slot],
            recv_sem=d_recv.at[slot],
            device_id={"inner": r - 1},
            device_id_type=MESH,
        )

    def copy_f(j):
        return pltpu.make_async_remote_copy(
            src_ref=fsend.at[j],
            dst_ref=frecv.at[j],
            send_sem=f_send.at[j],
            recv_sem=f_recv.at[j],
            device_id={"head": other},
            device_id_type=MESH,
        )

    barrier = pltpu.get_barrier_semaphore()
    pl.semaphore_signal(barrier, inc=1, device_id={"head": other}, device_id_type=MESH)

    @pl.when(has_prev)
    def _():
        pl.semaphore_signal(barrier, inc=1, device_id={"inner": r - 1}, device_id_type=MESH)

    @pl.when(has_next)
    def _():
        pl.semaphore_signal(barrier, inc=1, device_id={"inner": r + 1}, device_id_type=MESH)

    small = [
        pltpu.make_async_copy(source, target, in_sem.at[n])
        for n, (source, target) in enumerate(
            (
                (ke_hbm, ke_ref),
                (ve_hbm, ve_ref),
                (km_hbm, km_ref),
                (vm_hbm, vm_ref),
                (reach_hbm, reach_ref),
            )
        )
    ]
    for copy in small:
        copy.start()
    for slot in range(heads):
        load_q(slot).start()
        load_do(slot).start()
    for copy in small:
        copy.wait()

    half = length // 2
    for j in range(mine):
        for b in range(2):
            for which, mant, exps in ((0, km_ref, ke_ref), (1, vm_ref, ve_ref)):
                block = mant[0, 0, b * half : (b + 1) * half, j * D : (j + 1) * D].astype(F32)
                kv[j, which, length + b * half : length + (b + 1) * half, :] = (
                    block * scale_of(exps[0, 0, b, j])
                ).astype(BF16)

    pl.semaphore_wait(barrier, 1 + has_prev.astype(jnp.int32) + has_next.astype(jnp.int32))

    for j in range(mine):

        @pl.when(has_next)
        def _():
            copy_b(j).start()

    copy_a(0).start()

    key_at = lax.broadcasted_iota(jnp.int32, (length, 2 * rows), 0)
    query_at = lax.rem(lax.broadcasted_iota(jnp.int32, (length, 2 * rows), 1), rows) + h * rows
    first_seen = jnp.where(has_prev, length - reach_ref[0, 0], length)
    bias[0:length, :] = jnp.where(key_at >= first_seen, 0.0, NEG_FILL).astype(F32)
    bias[length : 2 * length, :] = jnp.where(key_at <= query_at, 0.0, NEG_FILL).astype(F32)

    @pl.when(jnp.logical_not(has_prev))
    def _():
        for slot in range(heads):
            kv[slot, :, 0:length, :] = jnp.zeros((2, length, D), BF16)

    @pl.when(jnp.logical_not(has_next))
    def _():
        grecv[...] = jnp.zeros_like(grecv)

    def pass_on(j):
        copy_a(j).wait_recv()

        @pl.when(has_next)
        def _():
            copy_b(mine + j).start()

    def finish(j):
        @pl.when(has_next)
        def _():
            copy_d(mine + j).wait_recv()

        fsend[j] = (own[mine + j] + grecv[mine + j].astype(F32)).astype(BF16)
        copy_f(j).start()

    chunk = 64
    chunks = 2 * length // chunk
    wide = 2 * rows
    pairs = GROUP // 2
    contract = (((1,), (1,)), ((), ()))

    def fold(x, op):
        folded = x[0:8]
        for at in range(8, x.shape[0], 8):
            folded = op(folded, x[at : at + 8])
        return folded

    def one_step(step, carry):
        slot = step + (step + heads - 2) // (heads - 1) - (heads - 1) * (step // (heads - 1))
        load_q(slot).wait()
        load_do(slot).wait()

        @pl.when(step == 0)
        def _():
            copy_a(0).wait_send()
            copy_a(1).start()

        @pl.when(step == 1)
        def _():
            pass_on(1)

        @pl.when(has_prev)
        def _():
            copy_b(slot).wait_recv()

        for n in range(GROUP):
            q_st[n] = q_s[slot, :, n * D : (n + 1) * D]
            do_st[n] = do_s[slot, :, n * D : (n + 1) * D]

        def products(pair, here):
            q_pair = q_st[pl.ds(2 * pair, 2)].reshape(wide, D)
            do_pair = do_st[pl.ds(2 * pair, 2)].reshape(wide, D)
            s_buf[here] = lax.dot_general(
                kv[slot, 0], q_pair, contract, preferred_element_type=F32
            )
            dp_buf[here] = lax.dot_general(
                kv[slot, 1], do_pair, contract, preferred_element_type=F32
            )

        def softmax(pair, here):
            peak = None
            for c in range(chunks):
                at = slice(c * chunk, (c + 1) * chunk)
                x = s_buf[here, at] * (factor * LOG2E) + bias[at]
                s_buf[here, at] = x
                some = fold(x, jnp.maximum)
                peak = some if peak is None else jnp.maximum(peak, some)
            peak = jnp.max(peak, axis=0, keepdims=True)
            total = None
            for c in range(chunks):
                at = slice(c * chunk, (c + 1) * chunk)
                x = jnp.exp2(s_buf[here, at] - peak)
                s_buf[here, at] = x
                some = fold(x, jnp.add)
                total = some if total is None else total + some
            inverse = 1.0 / jnp.sum(total, axis=0, keepdims=True)
            row_dot = None
            for c in range(chunks):
                at = slice(c * chunk, (c + 1) * chunk)
                rounded = (s_buf[here, at] * inverse).astype(BF16)
                p_s[pair, at] = rounded
                some = fold(rounded.astype(F32) * dp_buf[here, at], jnp.add)
                row_dot = some if row_dot is None else row_dot + some
            row_dot = jnp.sum(row_dot, axis=0, keepdims=True)
            for c in range(chunks):
                at = slice(c * chunk, (c + 1) * chunk)
                x = (s_buf[here, at] * inverse) * (dp_buf[here, at] - row_dot)
                ds_s[pair, at] = x.astype(BF16)

        products(0, 0)

        def two_pairs(n, carry):
            products(2 * n + 1, 1)
            softmax(2 * n, 0)
            products(jnp.minimum(2 * n + 2, pairs - 1), 0)
            softmax(2 * n + 1, 1)

            @pl.when(jnp.logical_and(step == 0, n == 0))
            def _():
                pass_on(0)

            return carry

        lax.fori_loop(0, pairs // 2, two_pairs, 0)

        @pl.when(step == heads - 1)
        def _():
            finish(1)

        q_all = q_st[...].reshape(GROUP * rows, D)
        do_all = do_st[...].reshape(GROUP * rows, D)
        p_all = jnp.concatenate([p_s[n] for n in range(pairs)], axis=1)
        ds_all = jnp.concatenate([ds_s[n] for n in range(pairs)], axis=1)
        dv = jnp.dot(p_all, do_all, preferred_element_type=F32)
        gsend[slot, 1] = dv[:length].astype(BF16)
        own[slot, 1] = dv[length:]
        dk = jnp.dot(ds_all, q_all, preferred_element_type=F32) * factor
        gsend[slot, 0] = dk[:length].astype(BF16)

        @pl.when(has_prev)
        def _():
            copy_d(slot).start()

        own[slot, 0] = dk[length:]
        keys_t = kv[slot, 0].T
        base = pl.multiple_of(lax.rem(mine * h + slot, heads) * width, width)
        grad_t = jnp.dot(keys_t, ds_all, preferred_element_type=F32) * factor
        grad = grad_t.astype(BF16).T
        for n in range(GROUP):
            dq_ref[0, 0, :, pl.ds(base + n * D, D)] = grad[n * rows : (n + 1) * rows]

        @pl.when(step == heads - 2)
        def _():
            finish(0)

        return carry

    lax.fori_loop(0, heads, one_step, 0)

    for j in range(mine):

        @pl.when(has_next)
        def _():
            copy_d(j).wait_recv()

        copy_f(j).wait_recv()
        total = own[j] + grecv[j].astype(F32) + frecv[j].astype(F32)
        dk_ref[0, 0, :, j * D : (j + 1) * D] = total[0].astype(BF16)
        dv_ref[0, 0, :, j * D : (j + 1) * D] = total[1].astype(BF16)

    copy_a(1).wait_send()
    for j in range(mine):
        copy_f(j).wait_send()
    for slot in range(heads):
        @pl.when(has_next)
        def _():
            copy_b(slot).wait_send()

        @pl.when(has_prev)
        def _():
            copy_d(slot).wait_send()


def on_device(ring, query, dout, key_mant, value_mantissas, key_exps, value_exponents, reach):
    rows, length = query.shape[2], key_mant.shape[2]
    mine = key_mant.shape[3] // D
    heads = 2 * mine
    width = GROUP * D
    hbm = pl.BlockSpec(memory_space=pltpu.HBM)
    vmem = pl.BlockSpec(memory_space=pltpu.VMEM)
    dma = pltpu.SemaphoreType.DMA
    out_shape = (
        pltpu.VMEM(query.shape, BF16),
        pltpu.VMEM(key_mant.shape, BF16),
        pltpu.VMEM(key_mant.shape, BF16),
    )
    return pl.pallas_call(
        functools.partial(kernel, ring),
        out_shape=out_shape,
        in_specs=[hbm] * 7,
        out_specs=(vmem, vmem, vmem),
        scratch_shapes=[
            pltpu.VMEM((heads, rows, width), BF16),
            pltpu.VMEM((heads, rows, width), BF16),
            pltpu.VMEM(key_mant.shape, BF16),
            pltpu.VMEM(key_mant.shape, BF16),
            pltpu.SMEM(key_exps.shape, jnp.int32),
            pltpu.SMEM(key_exps.shape, jnp.int32),
            pltpu.SMEM(reach.shape, jnp.int32),
            pltpu.VMEM((heads, 2, 2 * length, D), BF16),
            pltpu.VMEM((2 * length, 2 * rows), F32),
            pltpu.VMEM((GROUP, rows, D), BF16),
            pltpu.VMEM((GROUP, rows, D), BF16),
            pltpu.VMEM((2, 2 * length, 2 * rows), F32),
            pltpu.VMEM((2, 2 * length, 2 * rows), F32),
            pltpu.VMEM((GROUP // 2, 2 * length, 2 * rows), BF16),
            pltpu.VMEM((GROUP // 2, 2 * length, 2 * rows), BF16),
            pltpu.VMEM((heads, 2, length, D), F32),
            pltpu.VMEM((heads, 2, length, D), BF16),
            pltpu.VMEM((heads, 2, length, D), BF16),
            pltpu.VMEM((mine, 2, length, D), BF16),
            pltpu.VMEM((mine, 2, length, D), BF16),
            dma((5,)),
            dma((heads,)),
            dma((heads,)),
            dma((mine,)),
            dma((mine,)),
            dma((heads,)),
            dma((heads,)),
            dma((heads,)),
            dma((heads,)),
            dma((mine,)),
            dma((mine,)),
        ],
        compiler_params=pltpu.CompilerParams(
            collective_id=0, has_side_effects=True, vmem_limit_bytes=56 * 2**20
        ),
        cost_estimate=pl.CostEstimate(
            flops=10 * heads * width * rows * 2 * length,
            bytes_accessed=6 * rows * heads * width,
            transcendentals=heads * GROUP * rows * 2 * length,
        ),
    )(query, dout, key_mant, value_mantissas, key_exps, value_exponents, reach)

def solution(mesh):
    assert mesh.shape["head"] == 2
    tokens = P("outer", "inner", "head", None)
    shared = P("outer", "inner", None, "head")
    return jax.shard_map(
        functools.partial(on_device, mesh.shape["inner"]),
        mesh=mesh,
        in_specs=(tokens, tokens, shared, shared, shared, shared, P("outer", "inner")),
        out_specs=(tokens, shared, shared),
        check_vma=False,
    )
```

```python
import functools

import jax
import jax.numpy as jnp
from jax import lax
from jax.experimental import pallas as pl
from jax.experimental.pallas import tpu as pltpu
from jax.sharding import PartitionSpec as P

D = 128
GROUP = 8
LOG2E = 1.4426950408889634
NEG_FILL = -1e30
F32 = jnp.float32
BF16 = jnp.bfloat16
MESH = pl.DeviceIdType.MESH


def scale_of(exponent):
    return jnp.where(exponent > 0, 2.0, jnp.where(exponent < 0, 0.5, 1.0)).astype(F32)


def kernel(
    ring,
    q_hbm,
    do_hbm,
    km_hbm,
    vm_hbm,
    ke_hbm,
    ve_hbm,
    reach_hbm,
    dq_ref,
    dk_ref,
    dv_ref,
    q_s,
    do_s,
    km_ref,
    vm_ref,
    ke_ref,
    ve_ref,
    reach_ref,
    kv,
    bias,
    q_st,
    do_st,
    s_buf,
    dp_buf,
    p_s,
    ds_s,
    own,
    gsend,
    grecv,
    fsend,
    frecv,
    in_sem,
    q_sem,
    do_sem,
    a_send,
    a_recv,
    b_send,
    b_recv,
    d_send,
    d_recv,
    f_send,
    f_recv,
):
    rows = q_s.shape[1]
    length = km_ref.shape[2]
    width = q_s.shape[2]
    mine = km_ref.shape[3] // D
    heads = 2 * mine
    factor = D**-0.5

    h = lax.axis_index("head")
    r = lax.axis_index("inner")
    other = 1 - h
    has_prev = r > 0
    has_next = r < ring - 1

    def columns(slot):
        return pl.ds(pl.multiple_of(lax.rem(mine * h + slot, heads) * width, width), width)

    def load_q(slot):
        return pltpu.make_async_copy(q_hbm.at[0, 0, :, columns(slot)], q_s.at[slot], q_sem.at[slot])

    def load_do(slot):
        return pltpu.make_async_copy(
            do_hbm.at[0, 0, :, columns(slot)], do_s.at[slot], do_sem.at[slot]
        )

    def copy_a(j):
        return pltpu.make_async_remote_copy(
            src_ref=kv.at[j, :, pl.ds(length, length)],
            dst_ref=kv.at[mine + j, :, pl.ds(length, length)],
            send_sem=a_send.at[j],
            recv_sem=a_recv.at[j],
            device_id={"head": other},
            device_id_type=MESH,
        )

    def copy_b(slot):
        return pltpu.make_async_remote_copy(
            src_ref=kv.at[slot, :, pl.ds(length, length)],
            dst_ref=kv.at[slot, :, pl.ds(0, length)],
            send_sem=b_send.at[slot],
            recv_sem=b_recv.at[slot],
            device_id={"inner": r + 1},
            device_id_type=MESH,
        )

    def copy_d(slot):
        return pltpu.make_async_remote_copy(
            src_ref=gsend.at[slot],
            dst_ref=grecv.at[slot],
            send_sem=d_send.at[slot],
            recv_sem=d_recv.at[slot],
            device_id={"inner": r - 1},
            device_id_type=MESH,
        )

    def copy_f(j):
        return pltpu.make_async_remote_copy(
            src_ref=fsend.at[j],
            dst_ref=frecv.at[j],
            send_sem=f_send.at[j],
            recv_sem=f_recv.at[j],
            device_id={"head": other},
            device_id_type=MESH,
        )

    barrier = pltpu.get_barrier_semaphore()
    pl.semaphore_signal(barrier, inc=1, device_id={"head": other}, device_id_type=MESH)

    @pl.when(has_prev)
    def _():
        pl.semaphore_signal(barrier, inc=1, device_id={"inner": r - 1}, device_id_type=MESH)

    @pl.when(has_next)
    def _():
        pl.semaphore_signal(barrier, inc=1, device_id={"inner": r + 1}, device_id_type=MESH)

    small = [
        pltpu.make_async_copy(source, target, in_sem.at[n])
        for n, (source, target) in enumerate(
            (
                (ke_hbm, ke_ref),
                (ve_hbm, ve_ref),
                (km_hbm, km_ref),
                (vm_hbm, vm_ref),
                (reach_hbm, reach_ref),
            )
        )
    ]
    for copy in small:
        copy.start()
    for slot in range(heads):
        load_q(slot).start()
        load_do(slot).start()
    for copy in small:
        copy.wait()

    half = length // 2
    for j in range(mine):
        for b in range(2):
            for which, mant, exps in ((0, km_ref, ke_ref), (1, vm_ref, ve_ref)):
                block = mant[0, 0, b * half : (b + 1) * half, j * D : (j + 1) * D].astype(F32)
                kv[j, which, length + b * half : length + (b + 1) * half, :] = (
                    block * scale_of(exps[0, 0, b, j])
                ).astype(BF16)

    pl.semaphore_wait(barrier, 1 + has_prev.astype(jnp.int32) + has_next.astype(jnp.int32))

    for j in range(mine):

        @pl.when(has_next)
        def _():
            copy_b(j).start()

    copy_a(0).start()

    key_at = lax.broadcasted_iota(jnp.int32, (length, 2 * rows), 0)
    query_at = lax.rem(lax.broadcasted_iota(jnp.int32, (length, 2 * rows), 1), rows) + h * rows
    first_seen = jnp.where(has_prev, length - reach_ref[0, 0], length)
    bias[0:length, :] = jnp.where(key_at >= first_seen, 0.0, NEG_FILL).astype(F32)
    bias[length : 2 * length, :] = jnp.where(key_at <= query_at, 0.0, NEG_FILL).astype(F32)

    @pl.when(jnp.logical_not(has_prev))
    def _():
        for slot in range(heads):
            kv[slot, :, 0:length, :] = jnp.zeros((2, length, D), BF16)

    @pl.when(jnp.logical_not(has_next))
    def _():
        grecv[...] = jnp.zeros_like(grecv)

    def pass_on(j):
        copy_a(j).wait_recv()

        @pl.when(has_next)
        def _():
            copy_b(mine + j).start()

    def finish(j):
        @pl.when(has_next)
        def _():
            copy_d(mine + j).wait_recv()

        fsend[j] = (own[mine + j] + grecv[mine + j].astype(F32)).astype(BF16)
        copy_f(j).start()

    chunk = 64
    chunks = 2 * length // chunk
    wide = 2 * rows
    pairs = GROUP // 2
    contract = (((1,), (1,)), ((), ()))

    def fold(x, op):
        folded = x[0:8]
        for at in range(8, x.shape[0], 8):
            folded = op(folded, x[at : at + 8])
        return folded

    def one_step(step, carry):
        slot = step + (step + heads - 2) // (heads - 1) - (heads - 1) * (step // (heads - 1))
        load_q(slot).wait()
        load_do(slot).wait()

        @pl.when(step == 0)
        def _():
            copy_a(0).wait_send()
            copy_a(1).start()

        @pl.when(has_prev)
        def _():
            copy_b(slot).wait_recv()

        for n in range(GROUP):
            q_st[n] = q_s[slot, :, n * D : (n + 1) * D]
            do_st[n] = do_s[slot, :, n * D : (n + 1) * D]

        def products(pair, here):
            q_pair = q_st[pl.ds(2 * pair, 2)].reshape(wide, D)
            do_pair = do_st[pl.ds(2 * pair, 2)].reshape(wide, D)
            s_buf[here] = lax.dot_general(
                kv[slot, 0], q_pair, contract, preferred_element_type=F32
            )
            dp_buf[here] = lax.dot_general(
                kv[slot, 1], do_pair, contract, preferred_element_type=F32
            )

        def softmax(pair, here):
            peak = None
            for c in range(chunks):
                at = slice(c * chunk, (c + 1) * chunk)
                x = s_buf[here, at] * (factor * LOG2E) + bias[at]
                s_buf[here, at] = x
                some = fold(x, jnp.maximum)
                peak = some if peak is None else jnp.maximum(peak, some)
            peak = jnp.max(peak, axis=0, keepdims=True)
            total = None
            for c in range(chunks):
                at = slice(c * chunk, (c + 1) * chunk)
                x = jnp.exp2(s_buf[here, at] - peak)
                s_buf[here, at] = x
                some = fold(x, jnp.add)
                total = some if total is None else total + some
            inverse = 1.0 / jnp.sum(total, axis=0, keepdims=True)
            row_dot = None
            for c in range(chunks):
                at = slice(c * chunk, (c + 1) * chunk)
                rounded = (s_buf[here, at] * inverse).astype(BF16)
                p_s[pair, at] = rounded
                some = fold(rounded.astype(F32) * dp_buf[here, at], jnp.add)
                row_dot = some if row_dot is None else row_dot + some
            row_dot = jnp.sum(row_dot, axis=0, keepdims=True)
            for c in range(chunks):
                at = slice(c * chunk, (c + 1) * chunk)
                x = (s_buf[here, at] * inverse) * (dp_buf[here, at] - row_dot)
                ds_s[pair, at] = x.astype(BF16)

        products(0, 0)

        def two_pairs(n, carry):
            products(2 * n + 1, 1)
            softmax(2 * n, 0)
            products(jnp.minimum(2 * n + 2, pairs - 1), 0)
            softmax(2 * n + 1, 1)

            for j in range(mine):

                @pl.when(jnp.logical_and(step == j, n == 0))
                def _():
                    pass_on(j)

            return carry

        lax.fori_loop(0, pairs // 2, two_pairs, 0)

        @pl.when(step == heads - 2)
        def _():
            finish(0)

        @pl.when(step == heads - 1)
        def _():
            finish(1)

        q_all = q_st[...].reshape(GROUP * rows, D)
        do_all = do_st[...].reshape(GROUP * rows, D)
        p_all = jnp.concatenate([p_s[n] for n in range(pairs)], axis=1)
        ds_all = jnp.concatenate([ds_s[n] for n in range(pairs)], axis=1)
        dv = jnp.dot(p_all, do_all, preferred_element_type=F32)
        gsend[slot, 1] = dv[:length].astype(BF16)
        own[slot, 1] = dv[length:]
        dk = jnp.dot(ds_all, q_all, preferred_element_type=F32) * factor
        gsend[slot, 0] = dk[:length].astype(BF16)

        @pl.when(has_prev)
        def _():
            copy_d(slot).start()

        own[slot, 0] = dk[length:]
        keys_t = kv[slot, 0].T
        base = pl.multiple_of(lax.rem(mine * h + slot, heads) * width, width)
        grad_t = jnp.dot(keys_t, ds_all, preferred_element_type=F32) * factor
        grad = grad_t.astype(BF16).T
        for n in range(GROUP):
            dq_ref[0, 0, :, pl.ds(base + n * D, D)] = grad[n * rows : (n + 1) * rows]

        return carry

    lax.fori_loop(0, heads, one_step, 0)

    for j in range(mine):

        @pl.when(has_next)
        def _():
            copy_d(j).wait_recv()

        copy_f(j).wait_recv()
        total = own[j] + grecv[j].astype(F32) + frecv[j].astype(F32)
        dk_ref[0, 0, :, j * D : (j + 1) * D] = total[0].astype(BF16)
        dv_ref[0, 0, :, j * D : (j + 1) * D] = total[1].astype(BF16)

    copy_a(1).wait_send()
    for j in range(mine):
        copy_f(j).wait_send()
    for slot in range(heads):
        @pl.when(has_next)
        def _():
            copy_b(slot).wait_send()

        @pl.when(has_prev)
        def _():
            copy_d(slot).wait_send()


def on_device(ring, query, dout, key_mant, value_mantissas, key_exps, value_exponents, reach):
    rows, length = query.shape[2], key_mant.shape[2]
    mine = key_mant.shape[3] // D
    heads = 2 * mine
    width = GROUP * D
    hbm = pl.BlockSpec(memory_space=pltpu.HBM)
    vmem = pl.BlockSpec(memory_space=pltpu.VMEM)
    dma = pltpu.SemaphoreType.DMA
    out_shape = (
        pltpu.VMEM(query.shape, BF16),
        pltpu.VMEM(key_mant.shape, BF16),
        pltpu.VMEM(key_mant.shape, BF16),
    )
    return pl.pallas_call(
        functools.partial(kernel, ring),
        out_shape=out_shape,
        in_specs=[hbm] * 7,
        out_specs=(vmem, vmem, vmem),
        scratch_shapes=[
            pltpu.VMEM((heads, rows, width), BF16),
            pltpu.VMEM((heads, rows, width), BF16),
            pltpu.VMEM(key_mant.shape, BF16),
            pltpu.VMEM(key_mant.shape, BF16),
            pltpu.SMEM(key_exps.shape, jnp.int32),
            pltpu.SMEM(key_exps.shape, jnp.int32),
            pltpu.SMEM(reach.shape, jnp.int32),
            pltpu.VMEM((heads, 2, 2 * length, D), BF16),
            pltpu.VMEM((2 * length, 2 * rows), F32),
            pltpu.VMEM((GROUP, rows, D), BF16),
            pltpu.VMEM((GROUP, rows, D), BF16),
            pltpu.VMEM((2, 2 * length, 2 * rows), F32),
            pltpu.VMEM((2, 2 * length, 2 * rows), F32),
            pltpu.VMEM((GROUP // 2, 2 * length, 2 * rows), BF16),
            pltpu.VMEM((GROUP // 2, 2 * length, 2 * rows), BF16),
            pltpu.VMEM((heads, 2, length, D), F32),
            pltpu.VMEM((heads, 2, length, D), BF16),
            pltpu.VMEM((heads, 2, length, D), BF16),
            pltpu.VMEM((mine, 2, length, D), BF16),
            pltpu.VMEM((mine, 2, length, D), BF16),
            dma((5,)),
            dma((heads,)),
            dma((heads,)),
            dma((mine,)),
            dma((mine,)),
            dma((heads,)),
            dma((heads,)),
            dma((heads,)),
            dma((heads,)),
            dma((mine,)),
            dma((mine,)),
        ],
        compiler_params=pltpu.CompilerParams(
            collective_id=0, has_side_effects=True, vmem_limit_bytes=56 * 2**20
        ),
        cost_estimate=pl.CostEstimate(
            flops=10 * heads * width * rows * 2 * length,
            bytes_accessed=6 * rows * heads * width,
            transcendentals=heads * GROUP * rows * 2 * length,
        ),
    )(query, dout, key_mant, value_mantissas, key_exps, value_exponents, reach)

def solution(mesh):
    assert mesh.shape["head"] == 2
    tokens = P("outer", "inner", "head", None)
    shared = P("outer", "inner", None, "head")
    return jax.shard_map(
        functools.partial(on_device, mesh.shape["inner"]),
        mesh=mesh,
        in_specs=(tokens, tokens, shared, shared, shared, shared, P("outer", "inner")),
        out_specs=(tokens, shared, shared),
        check_vma=False,
    )
```

```python
import functools

import jax
import jax.numpy as jnp
from jax import lax
from jax.experimental import pallas as pl
from jax.experimental.pallas import tpu as pltpu
from jax.sharding import PartitionSpec as P

D = 128
GROUP = 8
LOG2E = 1.4426950408889634
NEG_FILL = -1e30
F32 = jnp.float32
BF16 = jnp.bfloat16
MESH = pl.DeviceIdType.MESH


def scale_of(exponent):
    return jnp.where(exponent > 0, 2.0, jnp.where(exponent < 0, 0.5, 1.0)).astype(F32)


def kernel(
    ring,
    q_hbm,
    do_hbm,
    km_hbm,
    vm_hbm,
    ke_hbm,
    ve_hbm,
    reach_hbm,
    dq_ref,
    dk_ref,
    dv_ref,
    q_s,
    do_s,
    km_ref,
    vm_ref,
    ke_ref,
    ve_ref,
    reach_ref,
    kv,
    bias,
    q_t,
    do_t,
    s_buf,
    dp_buf,
    p_s,
    ds_s,
    own,
    gsend,
    grecv,
    fsend,
    frecv,
    in_sem,
    q_sem,
    do_sem,
    a_send,
    a_recv,
    b_send,
    b_recv,
    d_send,
    d_recv,
    f_send,
    f_recv,
):
    rows = q_s.shape[1]
    length = km_ref.shape[2]
    width = q_s.shape[2]
    mine = km_ref.shape[3] // D
    heads = 2 * mine
    factor = D**-0.5

    h = lax.axis_index("head")
    r = lax.axis_index("inner")
    other = 1 - h
    has_prev = r > 0
    has_next = r < ring - 1

    def columns(slot):
        return pl.ds(pl.multiple_of(lax.rem(mine * h + slot, heads) * width, width), width)

    def load_q(slot):
        return pltpu.make_async_copy(q_hbm.at[0, 0, :, columns(slot)], q_s.at[slot], q_sem.at[slot])

    def load_do(slot):
        return pltpu.make_async_copy(
            do_hbm.at[0, 0, :, columns(slot)], do_s.at[slot], do_sem.at[slot]
        )

    def copy_a(j):
        return pltpu.make_async_remote_copy(
            src_ref=kv.at[j, :, pl.ds(length, length)],
            dst_ref=kv.at[mine + j, :, pl.ds(length, length)],
            send_sem=a_send.at[j],
            recv_sem=a_recv.at[j],
            device_id={"head": other},
            device_id_type=MESH,
        )

    def copy_b(slot):
        return pltpu.make_async_remote_copy(
            src_ref=kv.at[slot, :, pl.ds(length, length)],
            dst_ref=kv.at[slot, :, pl.ds(0, length)],
            send_sem=b_send.at[slot],
            recv_sem=b_recv.at[slot],
            device_id={"inner": r + 1},
            device_id_type=MESH,
        )

    def copy_d(slot):
        return pltpu.make_async_remote_copy(
            src_ref=gsend.at[slot],
            dst_ref=grecv.at[slot],
            send_sem=d_send.at[slot],
            recv_sem=d_recv.at[slot],
            device_id={"inner": r - 1},
            device_id_type=MESH,
        )

    def copy_f(j):
        return pltpu.make_async_remote_copy(
            src_ref=fsend.at[j],
            dst_ref=frecv.at[j],
            send_sem=f_send.at[j],
            recv_sem=f_recv.at[j],
            device_id={"head": other},
            device_id_type=MESH,
        )

    barrier = pltpu.get_barrier_semaphore()
    pl.semaphore_signal(barrier, inc=1, device_id={"head": other}, device_id_type=MESH)

    @pl.when(has_prev)
    def _():
        pl.semaphore_signal(barrier, inc=1, device_id={"inner": r - 1}, device_id_type=MESH)

    @pl.when(has_next)
    def _():
        pl.semaphore_signal(barrier, inc=1, device_id={"inner": r + 1}, device_id_type=MESH)

    small = [
        pltpu.make_async_copy(source, target, in_sem.at[n])
        for n, (source, target) in enumerate(
            (
                (ke_hbm, ke_ref),
                (ve_hbm, ve_ref),
                (km_hbm, km_ref),
                (vm_hbm, vm_ref),
                (reach_hbm, reach_ref),
            )
        )
    ]
    for copy in small:
        copy.start()
    for slot in range(heads):
        load_q(slot).start()
        load_do(slot).start()
    for copy in small:
        copy.wait()

    half = length // 2
    for j in range(mine):
        for b in range(2):
            for which, mant, exps in ((0, km_ref, ke_ref), (1, vm_ref, ve_ref)):
                block = mant[0, 0, b * half : (b + 1) * half, j * D : (j + 1) * D].astype(F32)
                kv[j, which, length + b * half : length + (b + 1) * half, :] = (
                    block * scale_of(exps[0, 0, b, j])
                ).astype(BF16)

    pl.semaphore_wait(barrier, 1 + has_prev.astype(jnp.int32) + has_next.astype(jnp.int32))

    for j in range(mine):

        @pl.when(has_next)
        def _():
            copy_b(j).start()

    copy_a(0).start()

    key_at = lax.broadcasted_iota(jnp.int32, (length, 2 * rows), 0)
    query_at = lax.rem(lax.broadcasted_iota(jnp.int32, (length, 2 * rows), 1), rows) + h * rows
    first_seen = jnp.where(has_prev, length - reach_ref[0, 0], length)
    bias[0:length, :] = jnp.where(key_at >= first_seen, 0.0, NEG_FILL).astype(F32)
    bias[length : 2 * length, :] = jnp.where(key_at <= query_at, 0.0, NEG_FILL).astype(F32)

    @pl.when(jnp.logical_not(has_prev))
    def _():
        for slot in range(heads):
            kv[slot, :, 0:length, :] = jnp.zeros((2, length, D), BF16)

    @pl.when(jnp.logical_not(has_next))
    def _():
        grecv[...] = jnp.zeros_like(grecv)

    def turn(slot, carry):
        load_q(slot).wait()
        load_do(slot).wait()
        for n in range(GROUP):
            at = slice(n * D, (n + 1) * D)
            to = slice(n * rows, (n + 1) * rows)
            q_t[slot, :, to] = q_s[slot, :, at].T
            do_t[slot, :, to] = do_s[slot, :, at].T
        return carry

    lax.fori_loop(0, heads, turn, 0)

    def pass_on(j):
        copy_a(j).wait_recv()

        @pl.when(has_next)
        def _():
            copy_b(mine + j).start()

    def finish(j):
        @pl.when(has_next)
        def _():
            copy_d(mine + j).wait_recv()

        fsend[j] = (own[mine + j] + grecv[mine + j].astype(F32)).astype(BF16)
        copy_f(j).start()

    chunk = 64
    chunks = 2 * length // chunk
    wide = 2 * rows
    pairs = GROUP // 2

    def fold(x, op):
        folded = x[0:8]
        for at in range(8, x.shape[0], 8):
            folded = op(folded, x[at : at + 8])
        return folded

    def one_step(step, carry):
        slot = step + (step + heads - 2) // (heads - 1) - (heads - 1) * (step // (heads - 1))
        @pl.when(step == 0)
        def _():
            copy_a(0).wait_send()
            copy_a(1).start()

        @pl.when(has_prev)
        def _():
            copy_b(slot).wait_recv()

        def stacked(ref):
            return jnp.concatenate(
                [ref[slot, :, n * D : (n + 1) * D] for n in range(GROUP)], axis=0
            )

        def products(pair, here):
            span = slice(pair * wide, (pair + 1) * wide)
            s_buf[here] = jnp.dot(kv[slot, 0], q_t[slot, :, span], preferred_element_type=F32)
            dp_buf[here] = jnp.dot(kv[slot, 1], do_t[slot, :, span], preferred_element_type=F32)

        def softmax(pair, here):
            peak = None
            for c in range(chunks):
                at = slice(c * chunk, (c + 1) * chunk)
                x = s_buf[here, at] * (factor * LOG2E) + bias[at]
                s_buf[here, at] = x
                some = fold(x, jnp.maximum)
                peak = some if peak is None else jnp.maximum(peak, some)
            peak = jnp.max(peak, axis=0, keepdims=True)
            total = None
            for c in range(chunks):
                at = slice(c * chunk, (c + 1) * chunk)
                x = jnp.exp2(s_buf[here, at] - peak)
                s_buf[here, at] = x
                some = fold(x, jnp.add)
                total = some if total is None else total + some
            inverse = 1.0 / jnp.sum(total, axis=0, keepdims=True)
            row_dot = None
            for c in range(chunks):
                at = slice(c * chunk, (c + 1) * chunk)
                rounded = (s_buf[here, at] * inverse).astype(BF16)
                p_s[pair, at] = rounded
                some = fold(rounded.astype(F32) * dp_buf[here, at], jnp.add)
                row_dot = some if row_dot is None else row_dot + some
            row_dot = jnp.sum(row_dot, axis=0, keepdims=True)
            for c in range(chunks):
                at = slice(c * chunk, (c + 1) * chunk)
                x = (s_buf[here, at] * inverse) * (dp_buf[here, at] - row_dot)
                ds_s[pair, at] = x.astype(BF16)

        products(0, 0)
        for pair in range(pairs):
            if pair + 1 < pairs:
                products(pair + 1, (pair + 1) % 2)
            softmax(pair, pair % 2)
            if pair == 1:
                for j in range(mine):

                    @pl.when(step == j)
                    def _():
                        pass_on(j)

        @pl.when(step == heads - 2)
        def _():
            finish(0)

        @pl.when(step == heads - 1)
        def _():
            finish(1)

        q_all = stacked(q_s)
        do_all = stacked(do_s)
        p_all = jnp.concatenate([p_s[n] for n in range(pairs)], axis=1)
        ds_all = jnp.concatenate([ds_s[n] for n in range(pairs)], axis=1)
        dv = jnp.dot(p_all, do_all, preferred_element_type=F32)
        gsend[slot, 1] = dv[:length].astype(BF16)
        own[slot, 1] = dv[length:]
        dk = jnp.dot(ds_all, q_all, preferred_element_type=F32) * factor
        gsend[slot, 0] = dk[:length].astype(BF16)

        @pl.when(has_prev)
        def _():
            copy_d(slot).start()

        own[slot, 0] = dk[length:]
        keys_t = kv[slot, 0].T
        base = pl.multiple_of(lax.rem(mine * h + slot, heads) * width, width)
        grad_t = jnp.dot(keys_t, ds_all, preferred_element_type=F32) * factor
        grad = grad_t.astype(BF16).T
        for n in range(GROUP):
            dq_ref[0, 0, :, pl.ds(base + n * D, D)] = grad[n * rows : (n + 1) * rows]

        return carry

    lax.fori_loop(0, heads, one_step, 0)

    for j in range(mine):

        @pl.when(has_next)
        def _():
            copy_d(j).wait_recv()

        copy_f(j).wait_recv()
        total = own[j] + grecv[j].astype(F32) + frecv[j].astype(F32)
        dk_ref[0, 0, :, j * D : (j + 1) * D] = total[0].astype(BF16)
        dv_ref[0, 0, :, j * D : (j + 1) * D] = total[1].astype(BF16)

    copy_a(1).wait_send()
    for j in range(mine):
        copy_f(j).wait_send()
    for slot in range(heads):
        @pl.when(has_next)
        def _():
            copy_b(slot).wait_send()

        @pl.when(has_prev)
        def _():
            copy_d(slot).wait_send()


def on_device(ring, query, dout, key_mant, value_mantissas, key_exps, value_exponents, reach):
    rows, length = query.shape[2], key_mant.shape[2]
    mine = key_mant.shape[3] // D
    heads = 2 * mine
    width = GROUP * D
    hbm = pl.BlockSpec(memory_space=pltpu.HBM)
    vmem = pl.BlockSpec(memory_space=pltpu.VMEM)
    dma = pltpu.SemaphoreType.DMA
    out_shape = (
        pltpu.VMEM(query.shape, BF16),
        pltpu.VMEM(key_mant.shape, BF16),
        pltpu.VMEM(key_mant.shape, BF16),
    )
    return pl.pallas_call(
        functools.partial(kernel, ring),
        out_shape=out_shape,
        in_specs=[hbm] * 7,
        out_specs=(vmem, vmem, vmem),
        scratch_shapes=[
            pltpu.VMEM((heads, rows, width), BF16),
            pltpu.VMEM((heads, rows, width), BF16),
            pltpu.VMEM(key_mant.shape, BF16),
            pltpu.VMEM(key_mant.shape, BF16),
            pltpu.SMEM(key_exps.shape, jnp.int32),
            pltpu.SMEM(key_exps.shape, jnp.int32),
            pltpu.SMEM(reach.shape, jnp.int32),
            pltpu.VMEM((heads, 2, 2 * length, D), BF16),
            pltpu.VMEM((2 * length, 2 * rows), F32),
            pltpu.VMEM((heads, D, GROUP * rows), BF16),
            pltpu.VMEM((heads, D, GROUP * rows), BF16),
            pltpu.VMEM((2, 2 * length, 2 * rows), F32),
            pltpu.VMEM((2, 2 * length, 2 * rows), F32),
            pltpu.VMEM((GROUP // 2, 2 * length, 2 * rows), BF16),
            pltpu.VMEM((GROUP // 2, 2 * length, 2 * rows), BF16),
            pltpu.VMEM((heads, 2, length, D), F32),
            pltpu.VMEM((heads, 2, length, D), BF16),
            pltpu.VMEM((heads, 2, length, D), BF16),
            pltpu.VMEM((mine, 2, length, D), BF16),
            pltpu.VMEM((mine, 2, length, D), BF16),
            dma((5,)),
            dma((heads,)),
            dma((heads,)),
            dma((mine,)),
            dma((mine,)),
            dma((heads,)),
            dma((heads,)),
            dma((heads,)),
            dma((heads,)),
            dma((mine,)),
            dma((mine,)),
        ],
        compiler_params=pltpu.CompilerParams(
            collective_id=0, has_side_effects=True, vmem_limit_bytes=56 * 2**20
        ),
        cost_estimate=pl.CostEstimate(
            flops=10 * heads * width * rows * 2 * length,
            bytes_accessed=6 * rows * heads * width,
            transcendentals=heads * GROUP * rows * 2 * length,
        ),
    )(query, dout, key_mant, value_mantissas, key_exps, value_exponents, reach)

def solution(mesh):
    assert mesh.shape["head"] == 2
    tokens = P("outer", "inner", "head", None)
    shared = P("outer", "inner", None, "head")
    return jax.shard_map(
        functools.partial(on_device, mesh.shape["inner"]),
        mesh=mesh,
        in_specs=(tokens, tokens, shared, shared, shared, shared, P("outer", "inner")),
        out_specs=(tokens, shared, shared),
        check_vma=False,
    )
```

```python
import functools

import jax
import jax.numpy as jnp
from jax import lax
from jax.experimental import pallas as pl
from jax.experimental.pallas import tpu as pltpu
from jax.sharding import PartitionSpec as P

D = 128
GROUP = 8
LOG2E = 1.4426950408889634
NEG_FILL = -1e30
F32 = jnp.float32
BF16 = jnp.bfloat16
MESH = pl.DeviceIdType.MESH


def scale_of(exponent):
    return jnp.where(exponent > 0, 2.0, jnp.where(exponent < 0, 0.5, 1.0)).astype(F32)


def kernel(
    ring,
    q_hbm,
    do_hbm,
    km_hbm,
    vm_hbm,
    ke_hbm,
    ve_hbm,
    reach_hbm,
    dq_ref,
    dk_ref,
    dv_ref,
    q_s,
    do_s,
    km_ref,
    vm_ref,
    ke_ref,
    ve_ref,
    reach_ref,
    kv,
    bias,
    q_t,
    do_t,
    s_buf,
    dp_buf,
    p_s,
    ds_s,
    own,
    gsend,
    grecv,
    fsend,
    frecv,
    in_sem,
    q_sem,
    do_sem,
    a_send,
    a_recv,
    b_send,
    b_recv,
    d_send,
    d_recv,
    f_send,
    f_recv,
):
    rows = q_s.shape[1]
    length = km_ref.shape[2]
    width = q_s.shape[2]
    mine = km_ref.shape[3] // D
    heads = 2 * mine
    factor = D**-0.5

    h = lax.axis_index("head")
    r = lax.axis_index("inner")
    other = 1 - h
    has_prev = r > 0
    has_next = r < ring - 1

    def columns(slot):
        return pl.ds(pl.multiple_of(lax.rem(mine * h + slot, heads) * width, width), width)

    def load_q(slot):
        return pltpu.make_async_copy(q_hbm.at[0, 0, :, columns(slot)], q_s.at[slot], q_sem.at[slot])

    def load_do(slot):
        return pltpu.make_async_copy(
            do_hbm.at[0, 0, :, columns(slot)], do_s.at[slot], do_sem.at[slot]
        )

    def copy_a(j):
        return pltpu.make_async_remote_copy(
            src_ref=kv.at[j, :, pl.ds(length, length)],
            dst_ref=kv.at[mine + j, :, pl.ds(length, length)],
            send_sem=a_send.at[j],
            recv_sem=a_recv.at[j],
            device_id={"head": other},
            device_id_type=MESH,
        )

    def copy_b(slot):
        return pltpu.make_async_remote_copy(
            src_ref=kv.at[slot, :, pl.ds(length, length)],
            dst_ref=kv.at[slot, :, pl.ds(0, length)],
            send_sem=b_send.at[slot],
            recv_sem=b_recv.at[slot],
            device_id={"inner": r + 1},
            device_id_type=MESH,
        )

    def copy_d(slot, which):
        return pltpu.make_async_remote_copy(
            src_ref=gsend.at[slot, which],
            dst_ref=grecv.at[slot, which],
            send_sem=d_send.at[slot, which],
            recv_sem=d_recv.at[slot, which],
            device_id={"inner": r - 1},
            device_id_type=MESH,
        )

    def copy_f(j, which):
        return pltpu.make_async_remote_copy(
            src_ref=fsend.at[j, which],
            dst_ref=frecv.at[j, which],
            send_sem=f_send.at[j, which],
            recv_sem=f_recv.at[j, which],
            device_id={"head": other},
            device_id_type=MESH,
        )

    barrier = pltpu.get_barrier_semaphore()
    pl.semaphore_signal(barrier, inc=1, device_id={"head": other}, device_id_type=MESH)

    @pl.when(has_prev)
    def _():
        pl.semaphore_signal(barrier, inc=1, device_id={"inner": r - 1}, device_id_type=MESH)

    @pl.when(has_next)
    def _():
        pl.semaphore_signal(barrier, inc=1, device_id={"inner": r + 1}, device_id_type=MESH)

    small = [
        pltpu.make_async_copy(source, target, in_sem.at[n])
        for n, (source, target) in enumerate(
            (
                (ke_hbm, ke_ref),
                (ve_hbm, ve_ref),
                (km_hbm, km_ref),
                (vm_hbm, vm_ref),
                (reach_hbm, reach_ref),
            )
        )
    ]
    for copy in small:
        copy.start()
    for slot in range(heads):
        load_q(slot).start()
        load_do(slot).start()
    for copy in small:
        copy.wait()

    half = length // 2
    for j in range(mine):
        for b in range(2):
            for which, mant, exps in ((0, km_ref, ke_ref), (1, vm_ref, ve_ref)):
                block = mant[0, 0, b * half : (b + 1) * half, j * D : (j + 1) * D].astype(F32)
                kv[j, which, length + b * half : length + (b + 1) * half, :] = (
                    block * scale_of(exps[0, 0, b, j])
                ).astype(BF16)

    pl.semaphore_wait(barrier, 1 + has_prev.astype(jnp.int32) + has_next.astype(jnp.int32))

    for j in range(mine):

        @pl.when(has_next)
        def _():
            copy_b(j).start()

    copy_a(0).start()

    key_at = lax.broadcasted_iota(jnp.int32, (length, 2 * rows), 0)
    query_at = lax.rem(lax.broadcasted_iota(jnp.int32, (length, 2 * rows), 1), rows) + h * rows
    first_seen = jnp.where(has_prev, length - reach_ref[0, 0], length)
    bias[0:length, :] = jnp.where(key_at >= first_seen, 0.0, NEG_FILL).astype(F32)
    bias[length : 2 * length, :] = jnp.where(key_at <= query_at, 0.0, NEG_FILL).astype(F32)

    @pl.when(jnp.logical_not(has_prev))
    def _():
        for slot in range(heads):
            kv[slot, :, 0:length, :] = jnp.zeros((2, length, D), BF16)

    @pl.when(jnp.logical_not(has_next))
    def _():
        grecv[...] = jnp.zeros_like(grecv)

    def turn(slot, carry):
        load_q(slot).wait()
        load_do(slot).wait()
        for n in range(GROUP):
            at = slice(n * D, (n + 1) * D)
            to = slice(n * rows, (n + 1) * rows)
            q_t[slot, :, to] = q_s[slot, :, at].T
            do_t[slot, :, to] = do_s[slot, :, at].T
        return carry

    lax.fori_loop(0, heads, turn, 0)

    def pass_on(j):
        copy_a(j).wait_recv()

        @pl.when(has_next)
        def _():
            copy_b(mine + j).start()

    def finish(j):
        for which in (1, 0):

            @pl.when(has_next)
            def _():
                copy_d(mine + j, which).wait_recv()

            fsend[j, which] = (own[mine + j, which] + grecv[mine + j, which].astype(F32)).astype(
                BF16
            )
            copy_f(j, which).start()

    chunk = 64
    chunks = 2 * length // chunk
    wide = 2 * rows
    pairs = GROUP // 2

    def fold(x, op):
        folded = x[0:8]
        for at in range(8, x.shape[0], 8):
            folded = op(folded, x[at : at + 8])
        return folded

    def one_step(step, carry):
        slot = step + (step + heads - 2) // (heads - 1) - (heads - 1) * (step // (heads - 1))
        @pl.when(step == 0)
        def _():
            copy_a(0).wait_send()
            copy_a(1).start()

        @pl.when(has_prev)
        def _():
            copy_b(slot).wait_recv()

        def stacked(ref):
            return jnp.concatenate(
                [ref[slot, :, n * D : (n + 1) * D] for n in range(GROUP)], axis=0
            )

        def products(pair, here):
            span = slice(pair * wide, (pair + 1) * wide)
            s_buf[here] = jnp.dot(kv[slot, 0], q_t[slot, :, span], preferred_element_type=F32)
            dp_buf[here] = jnp.dot(kv[slot, 1], do_t[slot, :, span], preferred_element_type=F32)

        def softmax(pair, here):
            peak = None
            for c in range(chunks):
                at = slice(c * chunk, (c + 1) * chunk)
                x = s_buf[here, at] * (factor * LOG2E) + bias[at]
                s_buf[here, at] = x
                some = fold(x, jnp.maximum)
                peak = some if peak is None else jnp.maximum(peak, some)
            peak = jnp.max(peak, axis=0, keepdims=True)
            total = None
            for c in range(chunks):
                at = slice(c * chunk, (c + 1) * chunk)
                x = jnp.exp2(s_buf[here, at] - peak)
                s_buf[here, at] = x
                some = fold(x, jnp.add)
                total = some if total is None else total + some
            inverse = 1.0 / jnp.sum(total, axis=0, keepdims=True)
            row_dot = None
            for c in range(chunks):
                at = slice(c * chunk, (c + 1) * chunk)
                rounded = (s_buf[here, at] * inverse).astype(BF16)
                p_s[pair, at] = rounded
                some = fold(rounded.astype(F32) * dp_buf[here, at], jnp.add)
                row_dot = some if row_dot is None else row_dot + some
            row_dot = jnp.sum(row_dot, axis=0, keepdims=True)
            for c in range(chunks):
                at = slice(c * chunk, (c + 1) * chunk)
                x = (s_buf[here, at] * inverse) * (dp_buf[here, at] - row_dot)
                ds_s[pair, at] = x.astype(BF16)

        products(0, 0)
        for pair in range(pairs):
            if pair + 1 < pairs:
                products(pair + 1, (pair + 1) % 2)
            softmax(pair, pair % 2)
            if pair == 1:
                for j in range(mine):

                    @pl.when(step == j)
                    def _():
                        pass_on(j)

        @pl.when(step == heads - 2)
        def _():
            finish(0)

        @pl.when(step == heads - 1)
        def _():
            finish(1)

        q_all = stacked(q_s)
        do_all = stacked(do_s)
        p_all = jnp.concatenate([p_s[n] for n in range(pairs)], axis=1)
        ds_all = jnp.concatenate([ds_s[n] for n in range(pairs)], axis=1)
        dv = jnp.dot(p_all, do_all, preferred_element_type=F32)
        gsend[slot, 1] = dv[:length].astype(BF16)

        @pl.when(has_prev)
        def _():
            copy_d(slot, 1).start()

        own[slot, 1] = dv[length:]
        dk = jnp.dot(ds_all, q_all, preferred_element_type=F32) * factor
        gsend[slot, 0] = dk[:length].astype(BF16)

        @pl.when(has_prev)
        def _():
            copy_d(slot, 0).start()

        own[slot, 0] = dk[length:]
        keys_t = kv[slot, 0].T
        base = pl.multiple_of(lax.rem(mine * h + slot, heads) * width, width)
        grad_t = jnp.dot(keys_t, ds_all, preferred_element_type=F32) * factor
        grad = grad_t.astype(BF16).T
        for n in range(GROUP):
            dq_ref[0, 0, :, pl.ds(base + n * D, D)] = grad[n * rows : (n + 1) * rows]

        return carry

    lax.fori_loop(0, heads, one_step, 0)

    for which, out_ref in ((1, dv_ref), (0, dk_ref)):
        for j in range(mine):

            @pl.when(has_next)
            def _():
                copy_d(j, which).wait_recv()

            copy_f(j, which).wait_recv()
            total = (
                own[j, which] + grecv[j, which].astype(F32) + frecv[j, which].astype(F32)
            )
            out_ref[0, 0, :, j * D : (j + 1) * D] = total.astype(BF16)

    copy_a(1).wait_send()
    for which in range(2):
        for j in range(mine):
            copy_f(j, which).wait_send()
        for slot in range(heads):

            @pl.when(has_prev)
            def _():
                copy_d(slot, which).wait_send()

    for slot in range(heads):

        @pl.when(has_next)
        def _():
            copy_b(slot).wait_send()


def on_device(ring, query, dout, key_mant, value_mantissas, key_exps, value_exponents, reach):
    rows, length = query.shape[2], key_mant.shape[2]
    mine = key_mant.shape[3] // D
    heads = 2 * mine
    width = GROUP * D
    hbm = pl.BlockSpec(memory_space=pltpu.HBM)
    vmem = pl.BlockSpec(memory_space=pltpu.VMEM)
    dma = pltpu.SemaphoreType.DMA
    out_shape = (
        pltpu.VMEM(query.shape, BF16),
        pltpu.VMEM(key_mant.shape, BF16),
        pltpu.VMEM(key_mant.shape, BF16),
    )
    return pl.pallas_call(
        functools.partial(kernel, ring),
        out_shape=out_shape,
        in_specs=[hbm] * 7,
        out_specs=(vmem, vmem, vmem),
        scratch_shapes=[
            pltpu.VMEM((heads, rows, width), BF16),
            pltpu.VMEM((heads, rows, width), BF16),
            pltpu.VMEM(key_mant.shape, BF16),
            pltpu.VMEM(key_mant.shape, BF16),
            pltpu.SMEM(key_exps.shape, jnp.int32),
            pltpu.SMEM(key_exps.shape, jnp.int32),
            pltpu.SMEM(reach.shape, jnp.int32),
            pltpu.VMEM((heads, 2, 2 * length, D), BF16),
            pltpu.VMEM((2 * length, 2 * rows), F32),
            pltpu.VMEM((heads, D, GROUP * rows), BF16),
            pltpu.VMEM((heads, D, GROUP * rows), BF16),
            pltpu.VMEM((2, 2 * length, 2 * rows), F32),
            pltpu.VMEM((2, 2 * length, 2 * rows), F32),
            pltpu.VMEM((GROUP // 2, 2 * length, 2 * rows), BF16),
            pltpu.VMEM((GROUP // 2, 2 * length, 2 * rows), BF16),
            pltpu.VMEM((heads, 2, length, D), F32),
            pltpu.VMEM((heads, 2, length, D), BF16),
            pltpu.VMEM((heads, 2, length, D), BF16),
            pltpu.VMEM((mine, 2, length, D), BF16),
            pltpu.VMEM((mine, 2, length, D), BF16),
            dma((5,)),
            dma((heads,)),
            dma((heads,)),
            dma((mine,)),
            dma((mine,)),
            dma((heads,)),
            dma((heads,)),
            dma((heads, 2)),
            dma((heads, 2)),
            dma((mine, 2)),
            dma((mine, 2)),
        ],
        compiler_params=pltpu.CompilerParams(
            collective_id=0, has_side_effects=True, vmem_limit_bytes=56 * 2**20
        ),
        cost_estimate=pl.CostEstimate(
            flops=10 * heads * width * rows * 2 * length,
            bytes_accessed=6 * rows * heads * width,
            transcendentals=heads * GROUP * rows * 2 * length,
        ),
    )(query, dout, key_mant, value_mantissas, key_exps, value_exponents, reach)

def solution(mesh):
    assert mesh.shape["head"] == 2
    tokens = P("outer", "inner", "head", None)
    shared = P("outer", "inner", None, "head")
    return jax.shard_map(
        functools.partial(on_device, mesh.shape["inner"]),
        mesh=mesh,
        in_specs=(tokens, tokens, shared, shared, shared, shared, P("outer", "inner")),
        out_specs=(tokens, shared, shared),
        check_vma=False,
    )
```
